256 devices in a mesh: rep: 2 (over core), fsdp: 32 (over y, z), tp: 4 (over x).
Axes of the slice: x: 4, y: 4, z: 8, core: 2. Of those that a mesh axis runs over, the one named last changes fastest.
Arguments:
- input_query: bfloat16 [4096, 8192], P(('rep', 'tp'), 'fsdp'), may hold values from -6 to 6
- grad_query: bfloat16 [4096, 8192], P('rep', 'tp'), may hold values from -0.125 to 0.125
- input_output: bfloat16 [4096, 8192], P(('rep', 'tp'), 'fsdp'), may hold values from -6 to 6
- grad_output: bfloat16 [4096, 8192], P('rep', 'tp'), may hold values from -0.125 to 0.125
- moment_query: bfloat16 [2, 8192, 8192], P('rep', 'fsdp', 'tp'), may hold values from -6 to 6
- moment_output: bfloat16 [2, 8192, 8192], P('rep', 'fsdp', 'tp'), may hold values from -6 to 6
- basis_query: bfloat16 [8192, 256], P('tp'), may hold values from -0.0625 to 0.0625
- basis_output: bfloat16 [8192, 256], P('tp'), may hold values from -0.0625 to 0.0625
Outputs:
- update_query: bfloat16 [8192, 8192], P('fsdp', 'tp')
- update_output: bfloat16 [8192, 8192], P('fsdp', 'tp')
- next_moment_query: bfloat16 [2, 8192, 8192], P('rep', 'fsdp', 'tp')
- next_moment_output: bfloat16 [2, 8192, 8192], P('rep', 'fsdp', 'tp')
The draws below stay inside these ranges and needn't reach their ends.
All inputs are finite; a program needn't handle non-finite values.
Results may differ from the reference program's by a relative error of at most 0.017.
Values may be sent and summed in bfloat16 or wider, within the bound.
No kernel may reach another device: no remote copies, remote signals or barrier semaphores. Data moves between devices by JAX's collectives and lax.ppermute only.
A program may use at most 128 MiB of HBM per device.

```python
import jax
import jax.numpy as jnp
from jax import lax

D = 8192
RANK = 256
TOK_DEV = 512
REPS = 2
TOKENS = 4096
N_TP = 4


def steps_of(own_key, shape, shards, smallest, top_value):
    factor_of = 1.0
    for position, shards_of in shards:
        heights = jax.random.uniform(jax.random.fold_in(jax.random.fold_in(own_key, 6), position), (shards_of,), jnp.float32, smallest / len(shards), top_value / len(shards))
        factor_of = factor_of * jnp.repeat(jnp.exp(heights), shape[position] // shards_of).reshape((-1,) + (1,) * (len(shape) - 1 - position))
    return factor_of


def scatter_about(key, dims, scale, most, pieces=(), dtype=jnp.bfloat16):
    array = scale * jax.random.normal(key, dims, jnp.float32)
    if pieces:
        array = array * steps_of(key, dims, pieces, -0.22, 0.18)
    return jnp.clip(array, -most, most).astype(dtype)


def setup_inputs(seed: int = 0) -> dict:
    key_list = jax.random.split(jax.random.key(seed), 9)
    input_query = scatter_about(key_list[0], (TOKENS, D), 1.0, 6.0, ((0, 8), (1, 32)))
    grad_query = scatter_about(key_list[1], (TOKENS, D), (TOK_DEV * N_TP) ** -0.5, 0.125, ((0, 2), (1, 4)))
    input_output = scatter_about(key_list[2], (TOKENS, D), 1.0, 6.0, ((0, 8), (1, 32)))
    grad_output = scatter_about(key_list[3], (TOKENS, D), (TOK_DEV * N_TP) ** -0.5, 0.125, ((0, 2), (1, 4)))
    moment_query = scatter_about(key_list[4], (REPS, D, D), 1.0, 6.0, ((0, 2), (1, 32), (2, 4)))
    moment_output = scatter_about(key_list[5], (REPS, D, D), 1.0, 6.0, ((0, 2), (1, 32), (2, 4)))
    basis_query = scatter_about(key_list[6], (D, RANK), D ** -0.5, 0.0625, ((0, 4),))
    basis_output = scatter_about(key_list[7], (D, RANK), D ** -0.5, 0.0625, ((0, 4),))
    return {"input_query": input_query, "grad_query": grad_query, "input_output": input_output, "grad_output": grad_output, "moment_query": moment_query, "moment_output": moment_output, "basis_query": basis_query, "basis_output": basis_output}


retain = 0.5
epsilon = 1e-06

def dion_step(inputs, grads, moment, basis):
    span = TOK_DEV * N_TP
    buffers = []
    power = jnp.zeros((D, RANK), jnp.float32)
    for replica in range(REPS):
        gradient = jnp.dot(inputs[replica * span:(replica + 1) * span].T.astype(jnp.float32), grads[replica * span:(replica + 1) * span].astype(jnp.float32), preferred_element_type=jnp.float32)
        buffer = (moment[replica].astype(jnp.float32) + gradient).astype(jnp.bfloat16)
        buffers.append(buffer)
        power = power + jnp.dot(buffer.astype(jnp.float32), basis.astype(jnp.float32), preferred_element_type=jnp.float32)
    gram = jnp.dot(power.T, power, precision=lax.Precision.HIGHEST)
    lower = jnp.linalg.cholesky(gram)
    ortho = jax.scipy.linalg.solve_triangular(lower, power.T, lower=True).T
    ortho_b = ortho.astype(jnp.bfloat16)
    right = jnp.zeros((D, RANK), jnp.float32)
    for buffer in buffers:
        right = right + jnp.dot(buffer.T.astype(jnp.float32), ortho_b.astype(jnp.float32), preferred_element_type=jnp.float32)
    basis_new = right / jnp.sqrt(lax.optimization_barrier(jnp.sum(right * right, axis=0)) + epsilon)
    scaling = D / RANK ** 0.5
    update = (scaling * jnp.dot(ortho, basis_new.T, precision=lax.Precision.HIGHEST)).astype(jnp.bfloat16)
    feedback = jnp.dot(ortho, right.T, precision=lax.Precision.HIGHEST)
    moment_new = jnp.stack([(buffer.astype(jnp.float32) - (1.0 - retain) / REPS * feedback).astype(jnp.bfloat16) for buffer in buffers])
    return (update, moment_new)

def reference(input_query, grad_query, input_output, grad_output, moment_query, moment_output, basis_query, basis_output):
    update_query, next_query = dion_step(input_query, grad_query, moment_query, basis_query)
    update_output, next_output = dion_step(input_output, grad_output, moment_output, basis_output)
    return (update_query, update_output, next_query, next_output)
```

```python
import jax
import jax.numpy as jnp
from jax import lax
from jax.sharding import PartitionSpec as P

D = 8192
RANK = 256
N_TP = 4
N_Y = 4
N_Z = 8

retain = 0.5
epsilon = 1e-06

Y_GROUPS = [[y * N_Z + z for y in range(N_Y)] for z in range(N_Z)]
Z_GROUPS = [[y * N_Z + z for z in range(N_Z)] for y in range(N_Y)]


def contract_rows(left, right):
    return lax.dot_general(
        left, right, (((0,), (0,)), ((), ())), preferred_element_type=jnp.float32
    )


def shift_tp(x, by):
    return lax.ppermute(x, "tp", [(i, (i + by) % N_TP) for i in range(N_TP)])


def swap_cores(x):
    return lax.ppermute(x, "rep", [(0, 1), (1, 0)])


def gather_tokens(x):
    me = lax.axis_index("tp")
    whole = jnp.zeros((N_TP,) + x.shape, x.dtype)
    parts = [x] + [shift_tp(x, by) for by in (1, 3, 2)]
    for part, by in zip(parts, (0, 1, 3, 2)):
        whole = lax.dynamic_update_index_in_dim(whole, part, (me - by) % N_TP, 0)
    return whole.reshape(N_TP * x.shape[0], x.shape[1])


def sum_tp(x):
    others = [shift_tp(x, by) for by in (1, 3, 2)]
    return (
        x.astype(jnp.float32)
        + others[0].astype(jnp.float32)
        + others[1].astype(jnp.float32)
        + others[2].astype(jnp.float32)
    )


def scatter_sum(x, groups):
    n = len(groups[0])
    pieces = lax.all_to_all(
        x.reshape(n, x.shape[0] // n, x.shape[1]), "fsdp", 0, 0, axis_index_groups=groups
    )
    return jnp.sum(pieces.astype(jnp.float32), axis=0).astype(jnp.bfloat16)


def gather(x, groups):
    n = len(groups[0])
    pieces = lax.all_to_all(
        jnp.broadcast_to(x[None], (n,) + x.shape), "fsdp", 0, 0, axis_index_groups=groups
    )
    return pieces.reshape(n * x.shape[0], x.shape[1])


def per_device(
    input_query,
    grad_query,
    input_output,
    grad_output,
    moment_query,
    moment_output,
    basis_query,
    basis_output,
):
    first = lax.axis_index("rep") == 0

    def split(pair):
        return jnp.where(first, pair[0], pair[1]), jnp.where(first, pair[1], pair[0])

    inputs = [gather_tokens(input_query), gather_tokens(input_output)]
    grads = [grad_query, grad_output]
    moments = [moment_query, moment_output]
    bases = [basis_query, basis_output]
    buffers = [
        (moments[w][0].astype(jnp.float32) + contract_rows(inputs[w], grads[w])).astype(
            jnp.bfloat16
        )
        for w in range(2)
    ]
    mine, other = split(
        [jnp.dot(buffers[w], bases[w], preferred_element_type=jnp.float32) for w in range(2)]
    )
    mine = mine + swap_cores(other.astype(jnp.bfloat16)).astype(jnp.float32)
    power = sum_tp(mine.astype(jnp.bfloat16))
    power_b = power.astype(jnp.bfloat16)
    powers_b = split([power_b, swap_cores(power_b)])
    mine, other = split([contract_rows(buffers[w], powers_b[w]) for w in range(2)])
    mine = (mine + swap_cores(other.astype(jnp.bfloat16)).astype(jnp.float32)).astype(jnp.bfloat16)
    raw = gather(gather(scatter_sum(scatter_sum(mine, Y_GROUPS), Z_GROUPS), Z_GROUPS), Y_GROUPS)

    basis = jnp.where(first, basis_query, basis_output)
    gram = sum_tp(contract_rows(basis, raw))
    lower = jnp.linalg.cholesky(gram)
    inverse = jax.scipy.linalg.solve_triangular(
        lower, jnp.eye(RANK, dtype=jnp.float32), lower=True
    )
    ortho = jnp.dot(power, inverse.T, precision=lax.Precision.HIGHEST)
    right = jnp.dot(raw, inverse.T.astype(jnp.bfloat16), preferred_element_type=jnp.float32)
    squares = sum_tp(jnp.sum(right * right, axis=0, keepdims=True))
    scale = D / RANK**0.5 / jnp.sqrt(squares + epsilon)
    ortho_b = ortho.astype(jnp.bfloat16)
    scaled_b = (ortho * scale).astype(jnp.bfloat16)
    right_b = right.astype(jnp.bfloat16)
    orthos = split([ortho_b, swap_cores(ortho_b)])
    scaled = split([scaled_b, swap_cores(scaled_b)])
    rights = split([right_b, swap_cores(right_b)])
    results = []
    for w in range(2):
        results.append(
            jnp.dot(scaled[w], rights[w].T, preferred_element_type=jnp.float32).astype(jnp.bfloat16)
        )
    for w in range(2):
        feedback = jnp.dot(orthos[w], rights[w].T, preferred_element_type=jnp.float32)
        results.append(
            (buffers[w].astype(jnp.float32) - (1.0 - retain) / 2 * feedback).astype(jnp.bfloat16)[
                None
            ]
        )
    return tuple(results)


def solution(mesh):
    in_specs = (
        P(("rep", "tp"), "fsdp"),
        P("rep", "tp"),
        P(("rep", "tp"), "fsdp"),
        P("rep", "tp"),
        P("rep", "fsdp", "tp"),
        P("rep", "fsdp", "tp"),
        P("tp", None),
        P("tp", None),
    )
    out_specs = (P("fsdp", "tp"), P("fsdp", "tp"), P("rep", "fsdp", "tp"), P("rep", "fsdp", "tp"))
    return jax.shard_map(
        per_device, mesh=mesh, in_specs=in_specs, out_specs=out_specs, check_vma=False
    )
```

```python
import functools

import jax
import jax.numpy as jnp
from jax import lax
from jax.experimental import pallas as pl
from jax.experimental.pallas import tpu as pltpu
from jax.sharding import PartitionSpec as P

D = 8192
RANK = 256
N_TP = 4
N_Y = 4
N_Z = 8
LANES = 128
BLOCK = 64
GROUP = 16
COLUMNS = 512

retain = 0.5
epsilon = 1e-06

Z_GROUPS = [[y * N_Z + z for z in range(N_Z)] for y in range(N_Y)]


def contract_rows(left, right, precision=None):
    return lax.dot_general(
        left,
        right,
        (((0,), (0,)), ((), ())),
        precision=precision,
        preferred_element_type=jnp.float32,
    )


def halves(x):
    high = x.astype(jnp.bfloat16)
    return high, (x - high.astype(jnp.float32)).astype(jnp.bfloat16)


def shift_tp(x, by):
    return lax.ppermute(x, "tp", [(i, (i + by) % N_TP) for i in range(N_TP)])


def shift_y(x, by):
    pairs = [
        (y * N_Z + z, (y + by) % N_Y * N_Z + z) for y in range(N_Y) for z in range(N_Z)
    ]
    return lax.ppermute(x, "fsdp", pairs)


def swap_cores(x):
    return lax.ppermute(x, "rep", [(0, 1), (1, 0)])


def from_all(x, shift):
    return [x] + [shift(x, by) for by in (1, 2, 3)]


def in_order(parts, me):
    n = len(parts)
    rows = parts[0].shape[0]
    whole = jnp.zeros((n,) + parts[0].shape, parts[0].dtype)
    for by in range(n):
        whole = lax.dynamic_update_index_in_dim(whole, parts[by], (me - by) % n, 0)
    return whole.reshape((n * rows,) + parts[0].shape[1:])


def total(parts):
    return functools.reduce(jnp.add, [part.astype(jnp.float32) for part in parts])


def first_kernel(index, *refs):
    for x, y, m, out in zip(refs[0:2], refs[2:4], refs[4:6], refs[6:8]):
        out[...] = m[0].astype(jnp.float32) + contract_rows(x[...], y[...])


def middle_kernel(index, *refs):
    for w in range(2):
        xa, xb, ya, yb, acc, out = refs[w::2]
        out[...] = (
            acc[...] + contract_rows(xa[...], ya[...]) + contract_rows(xb[...], yb[...])
        )


def last_kernel(index, *refs):
    for w in range(2):
        x, y, acc, basis, out, power = refs[w::2]
        buffer = (acc[...] + contract_rows(x[...], y[...])).astype(jnp.bfloat16)
        out[...] = buffer
        term = jnp.dot(buffer, basis[...], preferred_element_type=jnp.float32)

        @pl.when(pl.program_id(0) == 0)
        def _():
            power[...] = term

        @pl.when(pl.program_id(0) > 0)
        def _():
            power[...] += term


def token_kernel(body, index, operands, results, name):
    first = results[0][1].shape
    rows, width = first
    spec = {
        "x": lambda a: pl.BlockSpec(a.shape, lambda j, i: (0, 0)),
        "y0": lambda a: pl.BlockSpec((a.shape[0] // N_TP, COLUMNS), lambda j, i: (i[0], j)),
        "y1": lambda a: pl.BlockSpec((a.shape[0] // N_TP, COLUMNS), lambda j, i: (i[1], j)),
        "y2": lambda a: pl.BlockSpec((a.shape[0] // N_TP, COLUMNS), lambda j, i: (i[2], j)),
        "y3": lambda a: pl.BlockSpec((a.shape[0] // N_TP, COLUMNS), lambda j, i: (i[3], j)),
        "m": lambda a: pl.BlockSpec((1, rows, COLUMNS), lambda j, i: (0, 0, j)),
        "wide": lambda a: pl.BlockSpec((rows, COLUMNS), lambda j, i: (0, j)),
        "q": lambda a: pl.BlockSpec((COLUMNS, a.shape[1]), lambda j, i: (j, 0)),
    }
    arrays = [a for _, a in operands]
    return pl.pallas_call(
        body,
        grid_spec=pltpu.PrefetchScalarGridSpec(
            num_scalar_prefetch=1,
            grid=(width // COLUMNS,),
            in_specs=[spec[kind](a) for kind, a in operands],
            out_specs=[spec[kind](a) for kind, a in results],
        ),
        out_shape=[a for _, a in results],
        compiler_params=pltpu.CompilerParams(
            dimension_semantics=("arbitrary",), vmem_limit_bytes=24 << 20
        ),
        cost_estimate=pl.CostEstimate(
            flops=4 * rows * width * 512, bytes_accessed=12 << 20, transcendentals=0
        ),
        name=name,
    )(index, *arrays)


def make_buffers(inputs, grads, moments, bases):
    me = lax.axis_index("tp")
    index = jnp.stack([(me - by) % N_TP for by in range(N_TP)]).astype(jnp.int32)
    far = [shift_tp(x, 2) for x in inputs]
    near = [shift_tp(x, 1) for x in inputs] + [shift_tp(x, 3) for x in inputs]
    rows, width = inputs[0].shape[1], grads[0].shape[1]
    acc = jax.ShapeDtypeStruct((rows, width), jnp.float32)
    buffer = jax.ShapeDtypeStruct((rows, width), jnp.bfloat16)
    power = jax.ShapeDtypeStruct((rows, bases[0].shape[1]), jnp.float32)
    kinds = lambda kind, arrays: [(kind, a) for a in arrays]
    accs = token_kernel(
        first_kernel,
        index,
        kinds("x", inputs) + kinds("y0", grads) + kinds("m", moments),
        kinds("wide", [acc, acc]),
        "own_tokens",
    )
    accs = token_kernel(
        middle_kernel,
        index,
        kinds("x", near) + kinds("y1", grads) + kinds("y3", grads) + kinds("wide", accs),
        kinds("wide", [acc, acc]),
        "near_tokens",
    )
    out = token_kernel(
        last_kernel,
        index,
        kinds("x", far) + kinds("y2", grads) + kinds("wide", accs) + kinds("q", bases),
        kinds("wide", [buffer, buffer]) + kinds("x", [power, power]),
        "far_tokens",
    )
    return out[:2], out[2:]


def dot_halves(a, b, dims):
    (ah, al), (bh, bl) = halves(a), halves(b)
    dot = lambda x, y: lax.dot_general(
        x, y, (dims, ((), ())), preferred_element_type=jnp.float32
    )
    return dot(ah, bh) + (dot(ah, bl) + dot(al, bh))


def inverse_kernel(gram_ref, out_ref, work):
    n = RANK
    work[:, :n] = gram_ref[...]
    row = lax.broadcasted_iota(jnp.int32, (n, n), 0)
    lane = lax.broadcasted_iota(jnp.int32, (n, n), 1)
    work[:, n:] = jnp.where(row == lane, 1.0, 0.0)
    row = lax.broadcasted_iota(jnp.int32, (BLOCK, LANES), 0)
    lane = lax.broadcasted_iota(jnp.int32, (BLOCK, LANES), 1)
    for r0 in range(0, n, BLOCK):
        c0 = r0 // LANES * LANES
        q0 = r0 - c0
        rest = r0 + BLOCK
        a = work[r0:rest, c0 : c0 + LANES]
        w = jnp.where(lane == row + q0, 1.0, 0.0)
        for k0 in range(0, BLOCK, GROUP):
            columns = [
                jnp.broadcast_to(a[:, q0 + k : q0 + k + 1], (BLOCK, LANES))
                for k in range(k0, k0 + GROUP)
            ]
            for i in range(GROUP):
                k = k0 + i
                factor = jnp.where(row > k, columns[i] * (1.0 / columns[i][k : k + 1, :]), 0.0)
                for j in range(i + 1, GROUP):
                    columns[j] = columns[j] - factor * columns[j][k : k + 1, :]
                a = a - factor * a[k : k + 1, :]
                w = w - factor * w[k : k + 1, :]
        pivots = jnp.sum(jnp.where(lane == row + q0, a, 0.0), axis=1, keepdims=True)
        w = w * lax.rsqrt(pivots)
        end = (rest + LANES - 1) // LANES * LANES
        done = dot_halves(w, work[c0 : c0 + LANES, c0 : n + end], ((1,), (0,)))
        out_ref[r0:rest, :end] = done[:, n - c0 :]
        if end < n:
            out_ref[r0:rest, end:] = jnp.zeros((BLOCK, n - end), jnp.float32)
        if rest < n:
            d0 = rest // LANES * LANES
            term = dot_halves(done[:, d0 - c0 : n - c0], done[:, d0 - c0 :], ((0,), (0,)))
            work[rest:, d0 : n + end] = work[rest:, d0 : n + end] - term[rest - d0 :, :]


def inverse_factor(gram):
    return pl.pallas_call(
        inverse_kernel,
        out_shape=jax.ShapeDtypeStruct((RANK, RANK), jnp.float32),
        in_specs=[pl.BlockSpec(memory_space=pltpu.VMEM)],
        out_specs=pl.BlockSpec(memory_space=pltpu.VMEM),
        scratch_shapes=[pltpu.VMEM((RANK, 2 * RANK), jnp.float32)],
        compiler_params=pltpu.CompilerParams(vmem_limit_bytes=16 << 20),
        cost_estimate=pl.CostEstimate(
            flops=8 * 1000 * 1000 * 1000, bytes_accessed=1 << 20, transcendentals=0
        ),
        name="inverse_factor",
    )(gram)


def per_device(
    input_query,
    grad_query,
    input_output,
    grad_output,
    moment_query,
    moment_output,
    basis_query,
    basis_output,
):
    first = lax.axis_index("rep") == 0
    tp = lax.axis_index("tp")
    y = lax.axis_index("fsdp") // N_Z

    def split(pair):
        return jnp.where(first, pair[0], pair[1]), jnp.where(first, pair[1], pair[0])

    buffers, powers = make_buffers(
        [input_query, input_output],
        [grad_query, grad_output],
        [moment_query, moment_output],
        [basis_query, basis_output],
    )
    mine, other = split(powers)
    mine = mine + swap_cores(other.astype(jnp.bfloat16)).astype(jnp.float32)
    power = total(from_all(mine.astype(jnp.bfloat16), shift_tp))
    power_b = power.astype(jnp.bfloat16)
    powers_b = split([power_b, swap_cores(power_b)])

    rows = RANK // N_TP
    gram = lax.dynamic_slice_in_dim(
        contract_rows(power, power, lax.Precision.HIGHEST), tp * rows, rows, 0
    )
    mine, other = split([contract_rows(buffers[w], powers_b[w]) for w in range(2)])
    mine = mine + swap_cores(other.astype(jnp.bfloat16)).astype(jnp.float32)

    def quarter(x, by):
        return lax.dynamic_slice_in_dim(x, (y + by) % N_Y * (x.shape[0] // N_Y), x.shape[0] // N_Y, 0)

    packed = [
        jnp.concatenate([quarter(mine, by).astype(jnp.bfloat16), *halves(quarter(gram, by))])
        for by in (1, 2, 3)
    ]
    packed = [shift_y(x, by) for x, by in zip(packed, (1, 2, 3))]
    cut = mine.shape[0] // N_Y
    few = gram.shape[0] // N_Y
    mine = total([quarter(mine, 0)] + [x[:cut] for x in packed])
    gram = total(
        [quarter(gram, 0)]
        + [x[cut : cut + few] for x in packed]
        + [x[cut + few :] for x in packed]
    )

    exchange = lambda x: lax.all_to_all(x, "fsdp", 0, 0, axis_index_groups=Z_GROUPS)
    cut = cut // N_Z
    width = mine.shape[1]
    packed = jnp.concatenate(
        [mine.astype(jnp.bfloat16).reshape(N_Z, cut, width)]
        + [jnp.broadcast_to(x[None], (N_Z,) + x.shape) for x in halves(gram)],
        axis=1,
    )
    packed = exchange(packed).astype(jnp.float32)
    mine = jnp.sum(packed[:, :cut], axis=0).astype(jnp.bfloat16)
    gram = jnp.sum(packed[:, cut : cut + few] + packed[:, cut + few :], axis=0)

    gram = in_order(from_all(gram, shift_y), y)
    raw = exchange(jnp.broadcast_to(mine[None], (N_Z,) + mine.shape)).reshape(N_Z * cut, width)
    raw_parts = from_all(raw, shift_y)
    gram = in_order(from_all(gram, shift_tp), tp)
    inverse = inverse_factor(gram)
    raw = in_order(raw_parts, y)

    ortho = jnp.dot(power, inverse.T, precision=lax.Precision.HIGHEST)
    right = jnp.dot(raw, inverse.T.astype(jnp.bfloat16), preferred_element_type=jnp.float32)
    squares = total(from_all(jnp.sum(right * right, axis=0, keepdims=True), shift_tp))
    scale = D / RANK**0.5 / jnp.sqrt(squares + epsilon)
    ortho_b = ortho.astype(jnp.bfloat16)
    scaled_b = (ortho * scale).astype(jnp.bfloat16)
    right_b = right.astype(jnp.bfloat16)
    orthos = split([ortho_b, swap_cores(ortho_b)])
    rights = split([right_b, swap_cores(right_b)])
    scaled = split([scaled_b, swap_cores(scaled_b)])
    moments = []
    for w in range(2):
        feedback = jnp.dot(orthos[w], rights[w].T, preferred_element_type=jnp.float32)
        moments.append(
            (buffers[w].astype(jnp.float32) - (1.0 - retain) / 2 * feedback).astype(jnp.bfloat16)[
                None
            ]
        )
    updates = [
        jnp.dot(scaled[w], rights[w].T, preferred_element_type=jnp.float32).astype(jnp.bfloat16)
        for w in range(2)
    ]
    return (*updates, *moments)


def solution(mesh):
    in_specs = (
        P(("rep", "tp"), "fsdp"),
        P("rep", "tp"),
        P(("rep", "tp"), "fsdp"),
        P("rep", "tp"),
        P("rep", "fsdp", "tp"),
        P("rep", "fsdp", "tp"),
        P("tp", None),
        P("tp", None),
    )
    out_specs = (P("fsdp", "tp"), P("fsdp", "tp"), P("rep", "fsdp", "tp"), P("rep", "fsdp", "tp"))
    return jax.shard_map(
        per_device, mesh=mesh, in_specs=in_specs, out_specs=out_specs, check_vma=False
    )
```

```python
import functools

import jax
import jax.numpy as jnp
from jax import lax
from jax.experimental import pallas as pl
from jax.experimental.pallas import tpu as pltpu
from jax.sharding import PartitionSpec as P

D = 8192
RANK = 256
N_TP = 4
N_Y = 4
N_Z = 8
LANES = 128
COLUMNS = 512
BLOCK = 64
GROUP = 16

retain = 0.5
epsilon = 1e-06

Y_GROUPS = [[y * N_Z + z for y in range(N_Y)] for z in range(N_Z)]
Z_GROUPS = [[y * N_Z + z for z in range(N_Z)] for y in range(N_Y)]


def contract_rows(left, right, precision=None):
    return lax.dot_general(
        left,
        right,
        (((0,), (0,)), ((), ())),
        precision=precision,
        preferred_element_type=jnp.float32,
    )


def halves(x):
    high = x.astype(jnp.bfloat16)
    return high, (x - high.astype(jnp.float32)).astype(jnp.bfloat16)


def shift_tp(x, by):
    return lax.ppermute(x, "tp", [(i, (i + by) % N_TP) for i in range(N_TP)])


def shift_y(x, by):
    pairs = [
        (y * N_Z + z, (y + by) % N_Y * N_Z + z) for y in range(N_Y) for z in range(N_Z)
    ]
    return lax.ppermute(x, "fsdp", pairs)


def swap_cores(x):
    return lax.ppermute(x, "rep", [(0, 1), (1, 0)])


def from_all(x, shift):
    return [x] + [shift(x, by) for by in (1, 2, 3)]


def in_order(parts, me):
    n = len(parts)
    whole = jnp.zeros((n,) + parts[0].shape, parts[0].dtype)
    for by in range(n):
        whole = lax.dynamic_update_index_in_dim(whole, parts[by], (me - by) % n, 0)
    return whole.reshape((n * parts[0].shape[0],) + parts[0].shape[1:])


def total(parts):
    return functools.reduce(jnp.add, [part.astype(jnp.float32) for part in parts])


def tokens_by_distance(query, output):
    query_up = shift_tp(query, 1)
    output_down = shift_tp(output, 3)
    query_down = shift_tp(query, 3)
    output_up = shift_tp(output, 1)
    query_far = shift_tp(query_up, 1)
    output_far = shift_tp(output_down, 3)
    return [
        [query, query_up, query_far, query_down],
        [output, output_up, output_far, output_down],
    ]


def exchange(x, groups):
    return lax.all_to_all(x, "fsdp", 0, 0, axis_index_groups=groups)


def copies(x, n):
    return jnp.broadcast_to(x[None], (n,) + x.shape)


def whole(a):
    return pl.BlockSpec(a.shape, lambda *_: (0,) * len(a.shape), pipeline_mode=pl.Buffered(1))


def local_kernel(body, operands, results, name, **more):
    return pl.pallas_call(
        body,
        out_shape=results,
        compiler_params=pltpu.CompilerParams(vmem_limit_bytes=12 << 20),
        cost_estimate=pl.CostEstimate(flops=1 << 20, bytes_accessed=1 << 20, transcendentals=0),
        name=name,
        **more,
    )(*operands)


def token_blocks(body, index, small, grads, results, scratch, name):
    count = grads[0].shape[0] // N_TP
    block = lambda a: pl.BlockSpec((count, a.shape[1]), lambda s, i: (i[s], 0))
    return pl.pallas_call(
        body,
        grid_spec=pltpu.PrefetchScalarGridSpec(
            num_scalar_prefetch=1,
            grid=(N_TP,),
            in_specs=[whole(a) for a in small] + [block(a) for a in grads],
            out_specs=[
                pl.BlockSpec(a.shape, lambda *_, n=len(a.shape): (0,) * n) for a in results
            ],
            scratch_shapes=scratch,
        ),
        out_shape=results,
        compiler_params=pltpu.CompilerParams(
            dimension_semantics=("arbitrary",), vmem_limit_bytes=32 << 20
        ),
        cost_estimate=pl.CostEstimate(flops=1 << 20, bytes_accessed=1 << 20, transcendentals=0),
        name=name,
    )(index, *small, *grads)


def power_kernel(index, *refs):
    step = pl.program_id(0)
    for w in range(2):
        own, up, down, moment, basis, grad, far, near = refs[w::2]
        product = jnp.dot(grad[...], basis[...], preferred_element_type=jnp.float32)
        product = product.astype(jnp.bfloat16)

        @pl.when(step == 0)
        def _():
            far[...] = product
            near[...] = jnp.dot(moment[0], basis[...], preferred_element_type=jnp.float32)

        for at, tokens in ((1, own), (2, up), (3, down)):

            @pl.when(step == at)
            def _():
                near[...] += contract_rows(tokens[...], product)


def buffer_kernel(index, *refs):
    step = pl.program_id(0)
    for w in range(2):
        far, own, up, down, moment, grad, buffer, acc = refs[w::2]

        @pl.when(step == 0)
        def _():
            acc[...] = moment[0].astype(jnp.float32)

        for at, tokens in ((0, far), (1, own), (2, up), (3, down)):

            @pl.when(step == at)
            def _():
                turned = tokens[...].T
                for c in range(0, acc.shape[1], COLUMNS):
                    here = slice(c, c + COLUMNS)
                    acc[:, here] += jnp.dot(
                        turned, grad[:, here], preferred_element_type=jnp.float32
                    )

        @pl.when(step == N_TP - 1)
        def _():
            buffer[...] = acc[...].astype(jnp.bfloat16)


def pack_kernel(mine, other, gram, out):
    many, few = mine.shape[0] // N_Y, gram.shape[0] // N_Y
    for j in range(N_Y):
        rows = slice(j * many, (j + 1) * many)
        term = mine[rows].astype(jnp.float32) + other[rows].astype(jnp.float32)
        out[j, :many] = term.astype(jnp.bfloat16)
        out[j, many:] = gram[j * few : (j + 1) * few]


def sum_y_kernel(pieces, out):
    n, rows, _ = out.shape
    few = RANK // N_TP // N_Y
    many = rows - few
    add = lambda at, size: total([pieces[j, at : at + size] for j in range(N_Y)])
    gram = add(n * many, few).astype(jnp.bfloat16)
    for j in range(n):
        out[j, :many] = add(j * many, many).astype(jnp.bfloat16)
        out[j, many:] = gram


def sum_z_kernel(pieces, out, gram):
    many = out.shape[1]
    rows = total([pieces[j, :many] for j in range(N_Z)]).astype(jnp.bfloat16)
    for j in range(N_Z):
        out[j] = rows
    gram[...] = total([pieces[j, many:] for j in range(N_Z)])


def dot_halves(a, b, dims):
    (ah, al), (bh, bl) = halves(a), halves(b)
    dot = lambda x, y: lax.dot_general(
        x, y, (dims, ((), ())), preferred_element_type=jnp.float32
    )
    return dot(ah, bh) + (dot(ah, bl) + dot(al, bh))


def inverse_kernel(gram_ref, out_ref, work):
    n = RANK
    work[:, :n] = gram_ref[...]
    row = lax.broadcasted_iota(jnp.int32, (n, n), 0)
    lane = lax.broadcasted_iota(jnp.int32, (n, n), 1)
    work[:, n:] = jnp.where(row == lane, 1.0, 0.0)
    row = lax.broadcasted_iota(jnp.int32, (BLOCK, LANES), 0)
    lane = lax.broadcasted_iota(jnp.int32, (BLOCK, LANES), 1)
    for r0 in range(0, n, BLOCK):
        c0 = r0 // LANES * LANES
        q0 = r0 - c0
        rest = r0 + BLOCK
        a = work[r0:rest, c0 : c0 + LANES]
        w = jnp.where(lane == row + q0, 1.0, 0.0)
        for k0 in range(0, BLOCK, GROUP):
            columns = [
                jnp.broadcast_to(a[:, q0 + k : q0 + k + 1], (BLOCK, LANES))
                for k in range(k0, k0 + GROUP)
            ]
            for i in range(GROUP):
                k = k0 + i
                factor = jnp.where(row > k, columns[i] * (1.0 / columns[i][k : k + 1, :]), 0.0)
                for j in range(i + 1, GROUP):
                    columns[j] = columns[j] - factor * columns[j][k : k + 1, :]
                a = a - factor * a[k : k + 1, :]
                w = w - factor * w[k : k + 1, :]
        pivots = jnp.sum(jnp.where(lane == row + q0, a, 0.0), axis=1, keepdims=True)
        w = w * lax.rsqrt(pivots)
        end = (rest + LANES - 1) // LANES * LANES
        done = dot_halves(w, work[c0 : c0 + LANES, c0 : n + end], ((1,), (0,)))
        out_ref[r0:rest, :end] = done[:, n - c0 :]
        if end < n:
            out_ref[r0:rest, end:] = jnp.zeros((BLOCK, n - end), jnp.float32)
        if rest < n:
            d0 = rest // LANES * LANES
            term = dot_halves(done[:, d0 - c0 : n - c0], done[:, d0 - c0 :], ((0,), (0,)))
            work[rest:, d0 : n + end] = work[rest:, d0 : n + end] - term[rest - d0 :, :]


def inverse_factor(gram):
    return pl.pallas_call(
        inverse_kernel,
        out_shape=jax.ShapeDtypeStruct((RANK, RANK), jnp.float32),
        in_specs=[pl.BlockSpec(memory_space=pltpu.VMEM)],
        out_specs=pl.BlockSpec(memory_space=pltpu.VMEM),
        scratch_shapes=[pltpu.VMEM((RANK, 2 * RANK), jnp.float32)],
        compiler_params=pltpu.CompilerParams(vmem_limit_bytes=6 << 20),
        cost_estimate=pl.CostEstimate(
            flops=8 * 1000 * 1000 * 1000, bytes_accessed=1 << 20, transcendentals=0
        ),
        name="inverse_factor",
    )(gram)


def per_device(
    input_query,
    grad_query,
    input_output,
    grad_output,
    moment_query,
    moment_output,
    basis_query,
    basis_output,
):
    first = lax.axis_index("rep") == 0
    tp = lax.axis_index("tp")
    y = lax.axis_index("fsdp") // N_Z

    def split(pair):
        return jnp.where(first, pair[0], pair[1]), jnp.where(first, pair[1], pair[0])

    grads = [grad_query, grad_output]
    bases = [basis_query, basis_output]
    tokens = tokens_by_distance(input_query, input_output)

    index = jnp.stack([(tp - by) % N_TP for by in (2, 0, 1, 3)]).astype(jnp.int32)
    pairs = list(zip(*tokens))
    own, up, far, down = [list(pair) for pair in pairs]
    whole_moments = [moment_query, moment_output]
    rows = own[0].shape[1]
    shape = lambda r, c, dtype: jax.ShapeDtypeStruct((r, c), dtype)
    ahead = token_blocks(
        power_kernel,
        index,
        own + up + down + whole_moments + bases,
        grads,
        [shape(own[0].shape[0], RANK, jnp.bfloat16)] * 2 + [shape(rows, RANK, jnp.float32)] * 2,
        [],
        "power_terms",
    )
    powers = [ahead[2 + w] + contract_rows(far[w], ahead[w]) for w in range(2)]
    mine, other = split(powers)
    mine = mine + swap_cores(other.astype(jnp.bfloat16)).astype(jnp.float32)
    mine, far = lax.optimization_barrier((mine.astype(jnp.bfloat16), far))
    power = total(from_all(mine, shift_tp))
    power_b = power.astype(jnp.bfloat16)
    powers_b = split([power_b, swap_cores(power_b)])

    width = grads[0].shape[1]
    buffers = token_blocks(
        buffer_kernel,
        index,
        far + own + up + down + whole_moments,
        grads,
        [shape(rows, width, jnp.bfloat16)] * 2,
        [pltpu.VMEM((rows, width), jnp.float32)] * 2,
        "buffers",
    )
    mine, other = split(
        [contract_rows(buffers[w], powers_b[w]).astype(jnp.bfloat16) for w in range(2)]
    )
    other = swap_cores(other)

    width = mine.shape[1]
    many, few = mine.shape[0] // N_Y, RANK // N_TP // N_Y
    gram = lax.dynamic_slice_in_dim(
        contract_rows(power, power, lax.Precision.HIGHEST), tp * (RANK // N_TP), RANK // N_TP, 0
    ).astype(jnp.bfloat16)
    half = lambda *dims: jax.ShapeDtypeStruct(dims, jnp.bfloat16)
    packed = local_kernel(
        pack_kernel, [mine, other, gram], half(N_Y, many + few, width), "pack_quarters"
    )
    packed = exchange(packed, Y_GROUPS)
    many = many // N_Z
    packed = local_kernel(sum_y_kernel, [packed], half(N_Z, many + few, width), "sum_over_y")
    packed = exchange(packed, Z_GROUPS)
    mine, gram = local_kernel(
        sum_z_kernel,
        [packed],
        [half(N_Z, many, width), shape(few, width, jnp.float32)],
        "sum_over_z",
    )

    raw = exchange(mine, Z_GROUPS).reshape(N_Z * many, width)
    gram = in_order(from_all(gram, shift_y), y)
    gram = in_order(from_all(gram, shift_tp), tp)
    inverse = inverse_factor(gram)
    ortho = jnp.dot(power, inverse.T, precision=lax.Precision.HIGHEST)
    orthos = split([ortho, swap_cores(ortho)])
    raw = exchange(copies(raw, N_Y), Y_GROUPS).reshape(-1, width)

    right = jnp.dot(raw, inverse.T.astype(jnp.bfloat16), preferred_element_type=jnp.float32)
    sums = from_all(jnp.sum(right * right, axis=0, keepdims=True), shift_tp)
    right_b = right.astype(jnp.bfloat16)
    rights = split([right_b, swap_cores(right_b)])
    nexts = []
    for w in range(2):
        feedback = jnp.dot(
            orthos[w].astype(jnp.bfloat16), rights[w].T, preferred_element_type=jnp.float32
        )
        nexts.append(
            (buffers[w].astype(jnp.float32) - (1.0 - retain) / 2 * feedback).astype(jnp.bfloat16)[
                None
            ]
        )
    sums, nexts[0] = lax.optimization_barrier((sums, nexts[0]))
    scale = D / RANK**0.5 / jnp.sqrt(total(sums) + epsilon)
    scales = split([scale, swap_cores(scale)])
    scales, nexts[1] = lax.optimization_barrier((scales, nexts[1]))
    updates = [
        jnp.dot(
            (orthos[w] * scales[w]).astype(jnp.bfloat16),
            rights[w].T,
            preferred_element_type=jnp.float32,
        ).astype(jnp.bfloat16)
        for w in range(2)
    ]
    return (*updates, *nexts)


def solution(mesh):
    in_specs = (
        P(("rep", "tp"), "fsdp"),
        P("rep", "tp"),
        P(("rep", "tp"), "fsdp"),
        P("rep", "tp"),
        P("rep", "fsdp", "tp"),
        P("rep", "fsdp", "tp"),
        P("tp", None),
        P("tp", None),
    )
    out_specs = (P("fsdp", "tp"), P("fsdp", "tp"), P("rep", "fsdp", "tp"), P("rep", "fsdp", "tp"))
    return jax.shard_map(
        per_device, mesh=mesh, in_specs=in_specs, out_specs=out_specs, check_vma=False
    )
```

```python
import functools

import jax
import jax.numpy as jnp
from jax import lax
from jax.experimental import pallas as pl
from jax.experimental.pallas import tpu as pltpu
from jax.sharding import PartitionSpec as P

D = 8192
RANK = 256
N_TP = 4
N_Y = 4
N_Z = 8
LANES = 128
COLUMNS = 512
BLOCK = 64
GROUP = 16

retain = 0.5
epsilon = 1e-06

Y_GROUPS = [[y * N_Z + z for y in range(N_Y)] for z in range(N_Z)]
Z_GROUPS = [[y * N_Z + z for z in range(N_Z)] for y in range(N_Y)]


def contract_rows(left, right, precision=None):
    return lax.dot_general(
        left,
        right,
        (((0,), (0,)), ((), ())),
        precision=precision,
        preferred_element_type=jnp.float32,
    )


def halves(x):
    high = x.astype(jnp.bfloat16)
    return high, (x - high.astype(jnp.float32)).astype(jnp.bfloat16)


def shift_tp(x, by):
    return lax.ppermute(x, "tp", [(i, (i + by) % N_TP) for i in range(N_TP)])


def shift_y(x, by):
    pairs = [
        (y * N_Z + z, (y + by) % N_Y * N_Z + z) for y in range(N_Y) for z in range(N_Z)
    ]
    return lax.ppermute(x, "fsdp", pairs)


def swap_cores(x):
    return lax.ppermute(x, "rep", [(0, 1), (1, 0)])


def from_all(x, shift):
    return [x] + [shift(x, by) for by in (1, 2, 3)]


def in_order(parts, me):
    n = len(parts)
    whole = jnp.zeros((n,) + parts[0].shape, parts[0].dtype)
    for by in range(n):
        whole = lax.dynamic_update_index_in_dim(whole, parts[by], (me - by) % n, 0)
    return whole.reshape((n * parts[0].shape[0],) + parts[0].shape[1:])


def total(parts):
    return functools.reduce(jnp.add, [part.astype(jnp.float32) for part in parts])


def tokens_by_distance(query, output):
    query_up = shift_tp(query, 1)
    output_down = shift_tp(output, 3)
    query_down = shift_tp(query, 3)
    output_up = shift_tp(output, 1)
    query_far = shift_tp(query_up, 1)
    output_far = shift_tp(output_down, 3)
    return [
        [query, query_up, query_far, query_down],
        [output, output_up, output_far, output_down],
    ]


def exchange(x, groups):
    return lax.all_to_all(x, "fsdp", 0, 0, axis_index_groups=groups)


def whole(a):
    return pl.BlockSpec(a.shape, lambda *_: (0,) * len(a.shape), pipeline_mode=pl.Buffered(1))


def local_kernel(body, operands, results, name, **more):
    return pl.pallas_call(
        body,
        out_shape=results,
        compiler_params=pltpu.CompilerParams(vmem_limit_bytes=12 << 20),
        cost_estimate=pl.CostEstimate(flops=1 << 20, bytes_accessed=1 << 20, transcendentals=0),
        name=name,
        **more,
    )(*operands)


def token_blocks(body, index, small, grads, results, specs, scratch, cost, name):
    count = grads[0].shape[0] // N_TP
    block = lambda a: pl.BlockSpec((count, a.shape[1]), lambda s, i: (i[s], 0))
    return pl.pallas_call(
        body,
        grid_spec=pltpu.PrefetchScalarGridSpec(
            num_scalar_prefetch=1,
            grid=(N_TP,),
            in_specs=[whole(a) for a in small] + [block(a) for a in grads],
            out_specs=specs,
            scratch_shapes=scratch,
        ),
        out_shape=results,
        compiler_params=pltpu.CompilerParams(
            dimension_semantics=("arbitrary",), vmem_limit_bytes=56 << 20
        ),
        cost_estimate=pl.CostEstimate(flops=cost, bytes_accessed=1 << 20, transcendentals=0),
        name=name,
    )(index, *small, *grads)


def product_kernel(index, moment, basis, grad, product, near):
    term = jnp.dot(grad[...], basis[...], preferred_element_type=jnp.float32)
    product[...] = term.astype(jnp.bfloat16)

    @pl.when(pl.program_id(0) == 0)
    def _():
        near[...] = jnp.dot(moment[0], basis[...], preferred_element_type=jnp.float32)


def buffer_kernel(index, *refs):
    step = pl.program_id(0)
    for w in range(2):
        far, own, up, down, moment, grad, buffer, acc = refs[w::2]

        @pl.when(step == 0)
        def _():
            acc[...] = moment[0].astype(jnp.float32)

        for at, tokens in ((0, far), (1, own), (2, up), (3, down)):

            @pl.when(step == at)
            def _():
                turned = tokens[...].T
                for c in range(0, acc.shape[1], COLUMNS):
                    here = slice(c, c + COLUMNS)
                    acc[:, here] += jnp.dot(
                        turned, grad[:, here], preferred_element_type=jnp.float32
                    )

        @pl.when(step == N_TP - 1)
        def _():
            buffer[...] = acc[...].astype(jnp.bfloat16)


def near_kernel(index, *refs):
    for w in range(2):
        own, up, down, product_own, product_up, product_down, base, out = refs[w::2]
        out[...] = (
            base[...]
            + contract_rows(own[...], product_own[...])
            + contract_rows(up[...], product_up[...])
            + contract_rows(down[...], product_down[...])
        )


def far_kernel(index, *refs):
    mine, other = refs[6:]
    query, output = [
        near[...] + contract_rows(far[...], product[...])
        for far, product, near in (refs[0:6:2], refs[1:6:2])
    ]
    first = index[N_TP] == 0
    mine[...] = jnp.where(first, query, output)
    other[...] = jnp.where(first, output, query).astype(jnp.bfloat16)


def indexed_kernel(body, index, operands, results, name, grid=(1,), limit=16 << 20):
    spec = lambda block, place: pl.BlockSpec(block, place)
    return pl.pallas_call(
        body,
        grid_spec=pltpu.PrefetchScalarGridSpec(
            num_scalar_prefetch=1,
            grid=grid,
            in_specs=[spec(block, place) for _, block, place in operands],
            out_specs=[spec(block, place) for _, block, place in results],
        ),
        out_shape=[shape for shape, _, _ in results],
        compiler_params=pltpu.CompilerParams(
            dimension_semantics=("arbitrary",), vmem_limit_bytes=limit
        ),
        cost_estimate=pl.CostEstimate(flops=1 << 28, bytes_accessed=1 << 20, transcendentals=0),
        name=name,
    )(index, *[a for a, _, _ in operands])


def all_of(a):
    return (a, a.shape, lambda s, i: (0,) * len(a.shape))


def feedback_kernel(index, right_mine, right_other, *refs):
    first = index[N_TP] == 0
    sides = (right_mine[...], right_other[...])
    for w in range(2):
        ortho, buffer, out = refs[w::2]
        right = jnp.where(first, sides[w], sides[1 - w])
        term = lax.dot_general(
            ortho[...].astype(jnp.bfloat16),
            right,
            (((1,), (1,)), ((), ())),
            preferred_element_type=jnp.float32,
        )
        out[0] = (buffer[...].astype(jnp.float32) - (1.0 - retain) / 2 * term).astype(jnp.bfloat16)


def update_kernel(index, right_mine, right_other, *refs):
    first = index[N_TP] == 0
    sides = (right_mine[...], right_other[...])
    for w in range(2):
        ortho, scale, out = refs[w::2]
        right = jnp.where(first, sides[w], sides[1 - w])
        out[...] = lax.dot_general(
            (ortho[...] * scale[...]).astype(jnp.bfloat16),
            right,
            (((1,), (1,)), ((), ())),
            preferred_element_type=jnp.float32,
        ).astype(jnp.bfloat16)


def pack_kernel(mine, other, gram, out):
    many, few = mine.shape[0] // N_Y, gram.shape[0] // N_Y
    for j in range(N_Y):
        rows = slice(j * many, (j + 1) * many)
        term = mine[rows].astype(jnp.float32) + other[rows].astype(jnp.float32)
        out[j, :many] = term.astype(jnp.bfloat16)
        out[j, many:] = gram[j * few : (j + 1) * few]


def both_halves(x):
    high = x.astype(jnp.bfloat16).astype(jnp.float32)
    return jnp.concatenate([high, x - high], axis=0).astype(jnp.bfloat16)


def sum_y_kernel(pieces, out):
    few = RANK // N_Y // N_Z
    many = out.shape[1] - 2 * few
    add = lambda at, size: total([pieces[j, at : at + size] for j in range(N_Y)])
    gram = add(N_Z * many, N_Z * few)
    for j in range(N_Z):
        out[j, :many] = add(j * many, many).astype(jnp.bfloat16)
        out[j, many:] = both_halves(gram[j * few : (j + 1) * few])


def sum_z_kernel(pieces, out):
    few = RANK // N_Y // N_Z
    many = out.shape[1] - 2 * few
    rows = total([pieces[j, :many] for j in range(N_Z)]).astype(jnp.bfloat16)
    gram = total([pieces[j, many:] for j in range(N_Z)])
    gram = both_halves(gram[:few] + gram[few:])
    for j in range(N_Z):
        out[j, :many] = rows
        out[j, many:] = gram


def unpack_kernel(pieces, out, gram):
    few = RANK // N_Y // N_Z
    many = pieces.shape[1] - 2 * few
    for j in range(N_Z):
        rows = pieces[j, :many]
        for k in range(N_Y):
            out[k, j * many : (j + 1) * many] = rows
        pair = pieces[j, many:].astype(jnp.float32)
        gram[j * few : (j + 1) * few] = pair[:few] + pair[few:]


def dot_halves(a, b, dims):
    (ah, al), (bh, bl) = halves(a), halves(b)
    dot = lambda x, y: lax.dot_general(
        x, y, (dims, ((), ())), preferred_element_type=jnp.float32
    )
    return dot(ah, bh) + (dot(ah, bl) + dot(al, bh))


def inverse_kernel(gram_ref, out_ref, work):
    n = RANK
    work[:, :n] = gram_ref[...]
    row = lax.broadcasted_iota(jnp.int32, (n, n), 0)
    lane = lax.broadcasted_iota(jnp.int32, (n, n), 1)
    work[:, n:] = jnp.where(row == lane, 1.0, 0.0)
    row = lax.broadcasted_iota(jnp.int32, (BLOCK, LANES), 0)
    lane = lax.broadcasted_iota(jnp.int32, (BLOCK, LANES), 1)
    for r0 in range(0, n, BLOCK):
        c0 = r0 // LANES * LANES
        q0 = r0 - c0
        rest = r0 + BLOCK
        a = work[r0:rest, c0 : c0 + LANES]
        w = jnp.where(lane == row + q0, 1.0, 0.0)
        for k0 in range(0, BLOCK, GROUP):
            columns = [
                jnp.broadcast_to(a[:, q0 + k : q0 + k + 1], (BLOCK, LANES))
                for k in range(k0, k0 + GROUP)
            ]
            for i in range(GROUP):
                k = k0 + i
                factor = jnp.where(row > k, columns[i] * (1.0 / columns[i][k : k + 1, :]), 0.0)
                for j in range(i + 1, GROUP):
                    columns[j] = columns[j] - factor * columns[j][k : k + 1, :]
                a = a - factor * a[k : k + 1, :]
                w = w - factor * w[k : k + 1, :]
        pivots = jnp.sum(jnp.where(lane == row + q0, a, 0.0), axis=1, keepdims=True)
        w = w * lax.rsqrt(pivots)
        end = (rest + LANES - 1) // LANES * LANES
        done = dot_halves(w, work[c0 : c0 + LANES, c0 : n + end], ((1,), (0,)))
        out_ref[r0:rest, :end] = done[:, n - c0 :]
        if end < n:
            out_ref[r0:rest, end:] = jnp.zeros((BLOCK, n - end), jnp.float32)
        if rest < n:
            d0 = rest // LANES * LANES
            term = dot_halves(done[:, d0 - c0 : n - c0], done[:, d0 - c0 :], ((0,), (0,)))
            work[rest:, d0 : n + end] = work[rest:, d0 : n + end] - term[rest - d0 :, :]


def inverse_factor(gram):
    return pl.pallas_call(
        inverse_kernel,
        out_shape=jax.ShapeDtypeStruct((RANK, RANK), jnp.float32),
        in_specs=[pl.BlockSpec(memory_space=pltpu.VMEM)],
        out_specs=pl.BlockSpec(memory_space=pltpu.VMEM),
        scratch_shapes=[pltpu.VMEM((RANK, 2 * RANK), jnp.float32)],
        compiler_params=pltpu.CompilerParams(vmem_limit_bytes=6 << 20),
        cost_estimate=pl.CostEstimate(
            flops=8 * 1000 * 1000 * 1000, bytes_accessed=1 << 20, transcendentals=0
        ),
        name="inverse_factor",
    )(gram)


def per_device(
    input_query,
    grad_query,
    input_output,
    grad_output,
    moment_query,
    moment_output,
    basis_query,
    basis_output,
):
    first = lax.axis_index("rep") == 0
    tp = lax.axis_index("tp")
    y = lax.axis_index("fsdp") // N_Z

    def split(pair):
        return jnp.where(first, pair[0], pair[1]), jnp.where(first, pair[1], pair[0])

    grads = [grad_query, grad_output]
    bases = [basis_query, basis_output]
    tokens = tokens_by_distance(input_query, input_output)

    index = jnp.stack([(tp - by) % N_TP for by in (2, 0, 1, 3)] + [lax.axis_index("rep")])
    index = index.astype(jnp.int32)
    own, up, far, down = [list(pair) for pair in zip(*tokens)]
    rows, count = own[0].shape[1], own[0].shape[0]
    shape = lambda dtype, *dims: jax.ShapeDtypeStruct(dims, dtype)
    square = shape(jnp.float32, rows, RANK)
    moments = [moment_query, moment_output]
    products, bases_terms = [], []
    for w in range(2):
        grad = grads[w] if w == 0 else lax.optimization_barrier((grads[w], up[0], down[1]))[0]
        product, term = token_blocks(
            product_kernel,
            index,
            [moments[w], bases[w]],
            [grad],
            [shape(jnp.bfloat16, N_TP * count, RANK), square],
            [
                pl.BlockSpec((count, RANK), lambda s, i: (i[s], 0)),
                pl.BlockSpec(square.shape, lambda s, i: (0, 0)),
            ],
            [],
            1 << 20,
            "basis_products",
        )
        products.append(product)
        bases_terms.append(term)
    part = lambda a, at: (a, (count, RANK), lambda s, i: (i[at], 0))
    near = indexed_kernel(
        near_kernel,
        index,
        [all_of(a) for a in own + up + down]
        + [part(a, at) for at in (1, 2, 3) for a in products]
        + [all_of(a) for a in bases_terms],
        [all_of(square)] * 2,
        "near_tokens",
    )
    mine, other = indexed_kernel(
        far_kernel,
        index,
        [all_of(a) for a in far] + [part(a, 0) for a in products] + [all_of(a) for a in near],
        [all_of(square), all_of(shape(jnp.bfloat16, rows, RANK))],
        "far_tokens",
    )
    mine = mine + swap_cores(other).astype(jnp.float32)
    mine, far = lax.optimization_barrier((mine.astype(jnp.bfloat16), far))
    width = grads[0].shape[1]
    buffers = token_blocks(
        buffer_kernel,
        index,
        far + own + up + down + moments,
        grads,
        [shape(jnp.bfloat16, rows, width)] * 2,
        [pl.BlockSpec((rows, width), lambda s, i: (0, 0))] * 2,
        [pltpu.VMEM((rows, width), jnp.float32)] * 2,
        1 << 33,
        "buffers",
    )
    parts, buffers = lax.optimization_barrier((from_all(mine, shift_tp), buffers))
    power = total(parts)
    power_b = power.astype(jnp.bfloat16)
    powers_b = split([power_b, swap_cores(power_b)])
    mine, other = split(
        [contract_rows(buffers[w], powers_b[w]).astype(jnp.bfloat16) for w in range(2)]
    )
    other = swap_cores(other)

    width = mine.shape[1]
    many, few = mine.shape[0] // N_Y, RANK // N_Y
    gram = contract_rows(power, power, lax.Precision.HIGHEST).astype(jnp.bfloat16)
    half = lambda *dims: shape(jnp.bfloat16, *dims)
    packed = local_kernel(
        pack_kernel, [mine, other, gram], half(N_Y, many + few, width), "pack_quarters"
    )
    packed = exchange(packed, Y_GROUPS)
    sent = half(N_Z, (many + 2 * few) // N_Z, width)
    packed = local_kernel(sum_y_kernel, [packed], sent, "sum_over_y")
    packed = exchange(packed, Z_GROUPS)
    packed = local_kernel(sum_z_kernel, [packed], sent, "sum_over_z")

    packed = exchange(packed, Z_GROUPS)
    raw, gram = local_kernel(
        unpack_kernel,
        [packed],
        [half(N_Y, many, width), shape(jnp.float32, few, width)],
        "unpack_rows",
    )
    gram = in_order(from_all(gram, shift_y), y)
    inverse = inverse_factor(gram)
    ortho = jnp.dot(power, inverse.T, precision=lax.Precision.HIGHEST)
    orthos = split([ortho, swap_cores(ortho)])
    raw = exchange(raw, Y_GROUPS).reshape(-1, width)

    right = jnp.dot(raw, inverse.T.astype(jnp.bfloat16), preferred_element_type=jnp.float32)
    sums = from_all(jnp.sum(right * right, axis=0, keepdims=True), shift_tp)
    right_b = right.astype(jnp.bfloat16)
    rights = [right_b, swap_cores(right_b)]
    steps = grads[0].shape[1] // COLUMNS
    tall = lambda a: (a, (COLUMNS, a.shape[1]), lambda s, i: (s, 0))
    wide = lambda a: (a, (rows, COLUMNS), lambda s, i: (0, s))
    result = shape(jnp.bfloat16, 1, rows, grads[0].shape[1])
    nexts = indexed_kernel(
        feedback_kernel,
        index,
        [tall(a) for a in rights] + [all_of(a) for a in orthos] + [wide(a) for a in buffers],
        [(result, (1, rows, COLUMNS), lambda s, i: (0, 0, s))] * 2,
        "feedback",
        grid=(steps,),
    )
    sums, nexts = lax.optimization_barrier((sums, nexts))
    scale = D / RANK**0.5 / jnp.sqrt(total(sums) + epsilon)
    scales = split([scale, swap_cores(scale)])
    updates = indexed_kernel(
        update_kernel,
        index,
        [tall(a) for a in rights] + [all_of(a) for a in orthos] + [all_of(a) for a in scales],
        [wide(shape(jnp.bfloat16, rows, grads[0].shape[1]))] * 2,
        "updates",
        grid=(steps,),
    )
    return (*updates, *nexts)


def solution(mesh):
    in_specs = (
        P(("rep", "tp"), "fsdp"),
        P("rep", "tp"),
        P(("rep", "tp"), "fsdp"),
        P("rep", "tp"),
        P("rep", "fsdp", "tp"),
        P("rep", "fsdp", "tp"),
        P("tp", None),
        P("tp", None),
    )
    out_specs = (P("fsdp", "tp"), P("fsdp", "tp"), P("rep", "fsdp", "tp"), P("rep", "fsdp", "tp"))
    return jax.shard_map(
        per_device, mesh=mesh, in_specs=in_specs, out_specs=out_specs, check_vma=False
    )
```

```python
import functools

import jax
import jax.numpy as jnp
from jax import lax
from jax.experimental import pallas as pl
from jax.experimental.pallas import tpu as pltpu
from jax.sharding import PartitionSpec as P

D = 8192
RANK = 256
N_TP = 4
N_Y = 4
N_Z = 8
LANES = 128
BLOCK = 64
GROUP = 16

retain = 0.5
epsilon = 1e-06

Y_GROUPS = [[y * N_Z + z for y in range(N_Y)] for z in range(N_Z)]
Z_GROUPS = [[y * N_Z + z for z in range(N_Z)] for y in range(N_Y)]


def contract_rows(left, right, precision=None):
    return lax.dot_general(
        left,
        right,
        (((0,), (0,)), ((), ())),
        precision=precision,
        preferred_element_type=jnp.float32,
    )


def halves(x):
    high = x.astype(jnp.bfloat16)
    return high, (x - high.astype(jnp.float32)).astype(jnp.bfloat16)


def shift_tp(x, by):
    return lax.ppermute(x, "tp", [(i, (i + by) % N_TP) for i in range(N_TP)])


def shift_y(x, by):
    pairs = [
        (y * N_Z + z, (y + by) % N_Y * N_Z + z) for y in range(N_Y) for z in range(N_Z)
    ]
    return lax.ppermute(x, "fsdp", pairs)


def swap_cores(x):
    return lax.ppermute(x, "rep", [(0, 1), (1, 0)])


def from_all(x, shift):
    return [x] + [shift(x, by) for by in (1, 2, 3)]


def in_order(parts, me):
    n = len(parts)
    whole = jnp.zeros((n,) + parts[0].shape, parts[0].dtype)
    for by in range(n):
        whole = lax.dynamic_update_index_in_dim(whole, parts[by], (me - by) % n, 0)
    return whole.reshape((n * parts[0].shape[0],) + parts[0].shape[1:])


def total(parts):
    return functools.reduce(jnp.add, [part.astype(jnp.float32) for part in parts])


def tokens_by_distance(query, output):
    query_up = shift_tp(query, 1)
    output_down = shift_tp(output, 3)
    query_down = shift_tp(query, 3)
    output_up = shift_tp(output, 1)
    query_far = shift_tp(query_up, 1)
    output_far = shift_tp(output_down, 3)
    return [
        [query, query_up, query_far, query_down],
        [output, output_up, output_far, output_down],
    ]


def exchange(x, groups):
    return lax.all_to_all(x, "fsdp", 0, 0, axis_index_groups=groups)


def local_kernel(body, operands, results, name, cost=1 << 20):
    return pl.pallas_call(
        body,
        out_shape=results,
        compiler_params=pltpu.CompilerParams(vmem_limit_bytes=12 << 20),
        cost_estimate=pl.CostEstimate(flops=cost, bytes_accessed=1 << 20, transcendentals=0),
        name=name,
    )(*operands)


def near_kernel(index, *refs):
    for w in range(2):
        own, up, down, product_own, product_up, product_down, moment, basis, out = refs[w::2]
        out[...] = (
            jnp.dot(moment[0], basis[...], preferred_element_type=jnp.float32)
            + contract_rows(own[...], product_own[...])
            + contract_rows(up[...], product_up[...])
            + contract_rows(down[...], product_down[...])
        )


def far_kernel(index, *refs):
    mine, other = refs[6:]
    query, output = [
        near[...] + contract_rows(far[...], product[...])
        for far, product, near in (refs[0:6:2], refs[1:6:2])
    ]
    first = index[N_TP] == 0
    mine[...] = jnp.where(first, query, output)
    other[...] = jnp.where(first, output, query).astype(jnp.bfloat16)


def indexed_kernel(body, index, operands, results, name):
    spec = lambda block, place: pl.BlockSpec(block, place)
    return pl.pallas_call(
        body,
        grid_spec=pltpu.PrefetchScalarGridSpec(
            num_scalar_prefetch=1,
            grid=(1,),
            in_specs=[spec(block, place) for _, block, place in operands],
            out_specs=[spec(block, place) for _, block, place in results],
        ),
        out_shape=[shape for shape, _, _ in results],
        compiler_params=pltpu.CompilerParams(
            dimension_semantics=("arbitrary",), vmem_limit_bytes=24 << 20
        ),
        cost_estimate=pl.CostEstimate(flops=1 << 20, bytes_accessed=1 << 20, transcendentals=0),
        name=name,
    )(index, *[a for a, _, _ in operands])


def all_of(a):
    return (a, a.shape, lambda s, i: (0,) * len(a.shape))


def pack_kernel(mine, other, gram, out):
    many, few = mine.shape[0] // N_Y, gram.shape[0] // N_Y
    for j in range(N_Y):
        rows = slice(j * many, (j + 1) * many)
        term = mine[rows].astype(jnp.float32) + other[rows].astype(jnp.float32)
        out[j, :many] = term.astype(jnp.bfloat16)
        out[j, many:] = gram[j * few : (j + 1) * few]


def both_halves(x):
    high = x.astype(jnp.bfloat16).astype(jnp.float32)
    return jnp.concatenate([high, x - high], axis=0).astype(jnp.bfloat16)


def sum_y_kernel(pieces, out):
    few = RANK // N_Y // N_Z
    many = out.shape[1] - 2 * few
    add = lambda at, size: total([pieces[j, at : at + size] for j in range(N_Y)])
    gram = add(N_Z * many, N_Z * few)
    for j in range(N_Z):
        out[j, :many] = add(j * many, many).astype(jnp.bfloat16)
        out[j, many:] = both_halves(gram[j * few : (j + 1) * few])


def sum_z_kernel(pieces, out):
    few = RANK // N_Y // N_Z
    many = out.shape[1] - 2 * few
    rows = total([pieces[j, :many] for j in range(N_Z)]).astype(jnp.bfloat16)
    gram = total([pieces[j, many:] for j in range(N_Z)])
    gram = both_halves(gram[:few] + gram[few:])
    for j in range(N_Z):
        out[j, :many] = rows
        out[j, many:] = gram


def unpack_kernel(pieces, out, gram):
    few = RANK // N_Y // N_Z
    many = pieces.shape[1] - 2 * few
    for j in range(N_Z):
        rows = pieces[j, :many]
        for k in range(N_Y):
            out[k, j * many : (j + 1) * many] = rows
        pair = pieces[j, many:].astype(jnp.float32)
        gram[j * few : (j + 1) * few] = pair[:few] + pair[few:]


def dot_halves(a, b, dims):
    (ah, al), (bh, bl) = halves(a), halves(b)
    dot = lambda x, y: lax.dot_general(
        x, y, (dims, ((), ())), preferred_element_type=jnp.float32
    )
    return dot(ah, bh) + (dot(ah, bl) + dot(al, bh))


def inverse_kernel(gram_ref, out_ref, work):
    n = RANK
    work[:, :n] = gram_ref[...]
    row = lax.broadcasted_iota(jnp.int32, (n, n), 0)
    lane = lax.broadcasted_iota(jnp.int32, (n, n), 1)
    work[:, n:] = jnp.where(row == lane, 1.0, 0.0)
    row = lax.broadcasted_iota(jnp.int32, (BLOCK, LANES), 0)
    lane = lax.broadcasted_iota(jnp.int32, (BLOCK, LANES), 1)
    for r0 in range(0, n, BLOCK):
        c0 = r0 // LANES * LANES
        q0 = r0 - c0
        rest = r0 + BLOCK
        a = work[r0:rest, c0 : c0 + LANES]
        w = jnp.where(lane == row + q0, 1.0, 0.0)
        for k0 in range(0, BLOCK, GROUP):
            columns = [
                jnp.broadcast_to(a[:, q0 + k : q0 + k + 1], (BLOCK, LANES))
                for k in range(k0, k0 + GROUP)
            ]
            for i in range(GROUP):
                k = k0 + i
                factor = jnp.where(row > k, columns[i] * (1.0 / columns[i][k : k + 1, :]), 0.0)
                for j in range(i + 1, GROUP):
                    columns[j] = columns[j] - factor * columns[j][k : k + 1, :]
                a = a - factor * a[k : k + 1, :]
                w = w - factor * w[k : k + 1, :]
        pivots = jnp.sum(jnp.where(lane == row + q0, a, 0.0), axis=1, keepdims=True)
        w = w * lax.rsqrt(pivots)
        end = (rest + LANES - 1) // LANES * LANES
        done = dot_halves(w, work[c0 : c0 + LANES, c0 : n + end], ((1,), (0,)))
        out_ref[r0:rest, :end] = done[:, n - c0 :]
        if end < n:
            out_ref[r0:rest, end:] = jnp.zeros((BLOCK, n - end), jnp.float32)
        if rest < n:
            d0 = rest // LANES * LANES
            term = dot_halves(done[:, d0 - c0 : n - c0], done[:, d0 - c0 :], ((0,), (0,)))
            work[rest:, d0 : n + end] = work[rest:, d0 : n + end] - term[rest - d0 :, :]


def inverse_factor(gram):
    return pl.pallas_call(
        inverse_kernel,
        out_shape=jax.ShapeDtypeStruct((RANK, RANK), jnp.float32),
        in_specs=[pl.BlockSpec(memory_space=pltpu.VMEM)],
        out_specs=pl.BlockSpec(memory_space=pltpu.VMEM),
        scratch_shapes=[pltpu.VMEM((RANK, 2 * RANK), jnp.float32)],
        compiler_params=pltpu.CompilerParams(vmem_limit_bytes=6 << 20),
        cost_estimate=pl.CostEstimate(
            flops=8 * 1000 * 1000 * 1000, bytes_accessed=1 << 20, transcendentals=0
        ),
        name="inverse_factor",
    )(gram)


def per_device(
    input_query,
    grad_query,
    input_output,
    grad_output,
    moment_query,
    moment_output,
    basis_query,
    basis_output,
):
    first = lax.axis_index("rep") == 0
    tp = lax.axis_index("tp")
    y = lax.axis_index("fsdp") // N_Z

    def split(pair):
        return jnp.where(first, pair[0], pair[1]), jnp.where(first, pair[1], pair[0])

    grads = [grad_query, grad_output]
    bases = [basis_query, basis_output]
    tokens = tokens_by_distance(input_query, input_output)

    index = jnp.stack([(tp - by) % N_TP for by in (2, 0, 1, 3)] + [lax.axis_index("rep")])
    index = index.astype(jnp.int32)
    own, up, far, down = [list(pair) for pair in zip(*tokens)]
    rows, count = own[0].shape[1], own[0].shape[0]
    shape = lambda dtype, *dims: jax.ShapeDtypeStruct(dims, dtype)
    square = shape(jnp.float32, rows, RANK)
    moments = [moment_query, moment_output]
    products = []
    for w in range(2):
        grad = grads[w] if w == 0 else lax.optimization_barrier((grads[w], up[0], down[1]))[0]
        product = jnp.dot(grad, bases[w], preferred_element_type=jnp.float32)
        products.append(lax.optimization_barrier(product.astype(jnp.bfloat16)))
    part = lambda a, at: (a, (count, RANK), lambda s, i: (i[at], 0))
    near = indexed_kernel(
        near_kernel,
        index,
        [all_of(a) for a in own + up + down]
        + [part(a, at) for at in (1, 2, 3) for a in products]
        + [all_of(a) for a in moments + bases],
        [all_of(square)] * 2,
        "near_tokens",
    )
    mine, other = indexed_kernel(
        far_kernel,
        index,
        [all_of(a) for a in far] + [part(a, 0) for a in products] + [all_of(a) for a in near],
        [all_of(square), all_of(shape(jnp.bfloat16, rows, RANK))],
        "far_tokens",
    )
    mine = mine + swap_cores(other).astype(jnp.float32)
    mine, far = lax.optimization_barrier((mine.astype(jnp.bfloat16), far))
    buffers = [
        (
            moments[w][0].astype(jnp.float32)
            + contract_rows(in_order([own[w], up[w], far[w], down[w]], tp), grads[w])
        ).astype(jnp.bfloat16)
        for w in range(2)
    ]
    parts, buffers[0] = lax.optimization_barrier((from_all(mine, shift_tp), buffers[0]))
    power = total(parts)
    power_b = power.astype(jnp.bfloat16)
    powers_b = split([power_b, swap_cores(power_b)])
    mine, other = split(
        [contract_rows(buffers[w], powers_b[w]).astype(jnp.bfloat16) for w in range(2)]
    )
    other = swap_cores(other)

    width = mine.shape[1]
    many, few = mine.shape[0] // N_Y, RANK // N_Y
    gram = contract_rows(power, power, lax.Precision.HIGHEST).astype(jnp.bfloat16)
    half = lambda *dims: shape(jnp.bfloat16, *dims)
    packed = local_kernel(
        pack_kernel, [mine, other, gram], half(N_Y, many + few, width), "pack_quarters"
    )
    packed = exchange(packed, Y_GROUPS)
    sent = half(N_Z, (many + 2 * few) // N_Z, width)
    packed = local_kernel(sum_y_kernel, [packed], sent, "sum_over_y")
    packed = exchange(packed, Z_GROUPS)
    packed = local_kernel(sum_z_kernel, [packed], sent, "sum_over_z")

    packed = exchange(packed, Z_GROUPS)
    raw, gram = local_kernel(
        unpack_kernel,
        [packed],
        [half(N_Y, many, width), shape(jnp.float32, few, width)],
        "unpack_rows",
    )
    gram = in_order(from_all(gram, shift_y), y)
    inverse = inverse_factor(gram)
    ortho = jnp.dot(power, inverse.T, precision=lax.Precision.HIGHEST)
    orthos = split([ortho, swap_cores(ortho)])
    raw = exchange(raw, Y_GROUPS).reshape(-1, width)

    right = jnp.dot(raw, inverse.T.astype(jnp.bfloat16), preferred_element_type=jnp.float32)
    sums = from_all(jnp.sum(right * right, axis=0, keepdims=True), shift_tp)
    right_b = right.astype(jnp.bfloat16)
    rights = split([right_b, swap_cores(right_b)])
    nexts = []
    for w in range(2):
        feedback = jnp.dot(
            orthos[w].astype(jnp.bfloat16), rights[w].T, preferred_element_type=jnp.float32
        )
        nexts.append(
            (buffers[w].astype(jnp.float32) - (1.0 - retain) / 2 * feedback).astype(jnp.bfloat16)[
                None
            ]
        )
    sums, nexts[0] = lax.optimization_barrier((sums, nexts[0]))
    scale = D / RANK**0.5 / jnp.sqrt(total(sums) + epsilon)
    scales = split([scale, swap_cores(scale)])
    scales, nexts[1] = lax.optimization_barrier((scales, nexts[1]))
    updates = [
        jnp.dot(
            (orthos[w] * scales[w]).astype(jnp.bfloat16),
            rights[w].T,
            preferred_element_type=jnp.float32,
        ).astype(jnp.bfloat16)
        for w in range(2)
    ]
    return (*updates, *nexts)


def solution(mesh):
    in_specs = (
        P(("rep", "tp"), "fsdp"),
        P("rep", "tp"),
        P(("rep", "tp"), "fsdp"),
        P("rep", "tp"),
        P("rep", "fsdp", "tp"),
        P("rep", "fsdp", "tp"),
        P("tp", None),
        P("tp", None),
    )
    out_specs = (P("fsdp", "tp"), P("fsdp", "tp"), P("rep", "fsdp", "tp"), P("rep", "fsdp", "tp"))
    return jax.shard_map(
        per_device, mesh=mesh, in_specs=in_specs, out_specs=out_specs, check_vma=False
    )
```

```python
import functools

import jax
import jax.numpy as jnp
from jax import lax
from jax.experimental import pallas as pl
from jax.experimental.pallas import tpu as pltpu
from jax.sharding import PartitionSpec as P

D = 8192
RANK = 256
N_TP = 4
N_Y = 4
N_Z = 8
LANES = 128
BLOCK = 64
GROUP = 16

retain = 0.5
epsilon = 1e-06

Y_GROUPS = [[y * N_Z + z for y in range(N_Y)] for z in range(N_Z)]
Z_GROUPS = [[y * N_Z + z for z in range(N_Z)] for y in range(N_Y)]


def contract_rows(left, right, precision=None):
    return lax.dot_general(
        left,
        right,
        (((0,), (0,)), ((), ())),
        precision=precision,
        preferred_element_type=jnp.float32,
    )


def halves(x):
    high = x.astype(jnp.bfloat16)
    return high, (x - high.astype(jnp.float32)).astype(jnp.bfloat16)


def shift_tp(x, by):
    return lax.ppermute(x, "tp", [(i, (i + by) % N_TP) for i in range(N_TP)])


def shift_y(x, by):
    pairs = [
        (y * N_Z + z, (y + by) % N_Y * N_Z + z) for y in range(N_Y) for z in range(N_Z)
    ]
    return lax.ppermute(x, "fsdp", pairs)


def swap_cores(x):
    return lax.ppermute(x, "rep", [(0, 1), (1, 0)])


def from_all(x, shift):
    return [x] + [shift(x, by) for by in (1, 2, 3)]


def in_order(parts, me):
    n = len(parts)
    whole = jnp.zeros((n,) + parts[0].shape, parts[0].dtype)
    for by in range(n):
        whole = lax.dynamic_update_index_in_dim(whole, parts[by], (me - by) % n, 0)
    return whole.reshape((n * parts[0].shape[0],) + parts[0].shape[1:])


def total(parts):
    return functools.reduce(jnp.add, [part.astype(jnp.float32) for part in parts])


def tokens_by_distance(query, output):
    query_up = shift_tp(query, 1)
    output_down = shift_tp(output, 3)
    query_down = shift_tp(query, 3)
    output_up = shift_tp(output, 1)
    query_far = shift_tp(query_up, 1)
    output_far = shift_tp(output_down, 3)
    return [
        [query, query_up, query_far, query_down],
        [output, output_up, output_far, output_down],
    ]


def exchange(x, groups):
    return lax.all_to_all(x, "fsdp", 0, 0, axis_index_groups=groups)


def local_kernel(body, operands, results, name, cost=1 << 20):
    return pl.pallas_call(
        body,
        out_shape=results,
        compiler_params=pltpu.CompilerParams(vmem_limit_bytes=12 << 20),
        cost_estimate=pl.CostEstimate(flops=cost, bytes_accessed=1 << 20, transcendentals=0),
        name=name,
    )(*operands)


def near_kernel(index, *refs):
    for w in range(2):
        own, up, down, product_own, product_up, product_down, moment, basis, out = refs[w::2]
        out[...] = (
            jnp.dot(moment[0], basis[...], preferred_element_type=jnp.float32)
            + contract_rows(own[...], product_own[...])
            + contract_rows(up[...], product_up[...])
            + contract_rows(down[...], product_down[...])
        )


def far_kernel(index, *refs):
    mine, other = refs[6:]
    query, output = [
        near[...] + contract_rows(far[...], product[...])
        for far, product, near in (refs[0:6:2], refs[1:6:2])
    ]
    first = index[N_TP] == 0
    mine[...] = jnp.where(first, query, output)
    other[...] = jnp.where(first, output, query).astype(jnp.bfloat16)


def order_kernel(index, *refs):
    for w in range(2):
        far, own, up, down, out = refs[w::2]
        for at, tokens in enumerate((far, own, up, down)):
            out[pl.ds(index[at], 1)] = tokens[...][None]


def indexed_kernel(body, index, operands, results, name):
    spec = lambda block, place: pl.BlockSpec(block, place)
    return pl.pallas_call(
        body,
        grid_spec=pltpu.PrefetchScalarGridSpec(
            num_scalar_prefetch=1,
            grid=(1,),
            in_specs=[spec(block, place) for _, block, place in operands],
            out_specs=[spec(block, place) for _, block, place in results],
        ),
        out_shape=[shape for shape, _, _ in results],
        compiler_params=pltpu.CompilerParams(
            dimension_semantics=("arbitrary",), vmem_limit_bytes=24 << 20
        ),
        cost_estimate=pl.CostEstimate(flops=1 << 20, bytes_accessed=1 << 20, transcendentals=0),
        name=name,
    )(index, *[a for a, _, _ in operands])


def all_of(a):
    return (a, a.shape, lambda s, i: (0,) * len(a.shape))


def pack_kernel(mine, other, gram, out):
    many, few = mine.shape[0] // N_Y, gram.shape[0] // N_Y
    for j in range(N_Y):
        rows = slice(j * many, (j + 1) * many)
        term = mine[rows].astype(jnp.float32) + other[rows].astype(jnp.float32)
        out[j, :many] = term.astype(jnp.bfloat16)
        out[j, many:] = gram[j * few : (j + 1) * few]


def both_halves(x):
    high = x.astype(jnp.bfloat16).astype(jnp.float32)
    return jnp.concatenate([high, x - high], axis=0).astype(jnp.bfloat16)


def sum_y_kernel(pieces, out):
    few = RANK // N_Y // N_Z
    many = out.shape[1] - 2 * few
    add = lambda at, size: total([pieces[j, at : at + size] for j in range(N_Y)])
    gram = add(N_Z * many, N_Z * few)
    for j in range(N_Z):
        out[j, :many] = add(j * many, many).astype(jnp.bfloat16)
        out[j, many:] = both_halves(gram[j * few : (j + 1) * few])


def sum_z_kernel(pieces, out):
    few = RANK // N_Y // N_Z
    many = out.shape[1] - 2 * few
    rows = total([pieces[j, :many] for j in range(N_Z)]).astype(jnp.bfloat16)
    gram = total([pieces[j, many:] for j in range(N_Z)])
    gram = both_halves(gram[:few] + gram[few:])
    for j in range(N_Z):
        out[j, :many] = rows
        out[j, many:] = gram


def unpack_kernel(pieces, out, gram):
    few = RANK // N_Y // N_Z
    many = pieces.shape[1] - 2 * few
    for j in range(N_Z):
        rows = pieces[j, :many]
        for k in range(N_Y):
            out[k, j * many : (j + 1) * many] = rows
        pair = pieces[j, many:].astype(jnp.float32)
        gram[j * few : (j + 1) * few] = pair[:few] + pair[few:]


def dot_halves(a, b, dims):
    (ah, al), (bh, bl) = halves(a), halves(b)
    dot = lambda x, y: lax.dot_general(
        x, y, (dims, ((), ())), preferred_element_type=jnp.float32
    )
    return dot(ah, bh) + (dot(ah, bl) + dot(al, bh))


def inverse_kernel(gram_ref, out_ref, work):
    n = RANK
    work[:, :n] = gram_ref[...]
    row = lax.broadcasted_iota(jnp.int32, (n, n), 0)
    lane = lax.broadcasted_iota(jnp.int32, (n, n), 1)
    work[:, n:] = jnp.where(row == lane, 1.0, 0.0)
    row = lax.broadcasted_iota(jnp.int32, (BLOCK, LANES), 0)
    lane = lax.broadcasted_iota(jnp.int32, (BLOCK, LANES), 1)
    for r0 in range(0, n, BLOCK):
        c0 = r0 // LANES * LANES
        q0 = r0 - c0
        rest = r0 + BLOCK
        a = work[r0:rest, c0 : c0 + LANES]
        w = jnp.where(lane == row + q0, 1.0, 0.0)
        for k0 in range(0, BLOCK, GROUP):
            columns = [
                jnp.broadcast_to(a[:, q0 + k : q0 + k + 1], (BLOCK, LANES))
                for k in range(k0, k0 + GROUP)
            ]
            for i in range(GROUP):
                k = k0 + i
                factor = jnp.where(row > k, columns[i] * (1.0 / columns[i][k : k + 1, :]), 0.0)
                for j in range(i + 1, GROUP):
                    columns[j] = columns[j] - factor * columns[j][k : k + 1, :]
                a = a - factor * a[k : k + 1, :]
                w = w - factor * w[k : k + 1, :]
        pivots = jnp.sum(jnp.where(lane == row + q0, a, 0.0), axis=1, keepdims=True)
        w = w * lax.rsqrt(pivots)
        end = (rest + LANES - 1) // LANES * LANES
        done = dot_halves(w, work[c0 : c0 + LANES, c0 : n + end], ((1,), (0,)))
        out_ref[r0:rest, :end] = done[:, n - c0 :]
        if end < n:
            out_ref[r0:rest, end:] = jnp.zeros((BLOCK, n - end), jnp.float32)
        if rest < n:
            d0 = rest // LANES * LANES
            term = dot_halves(done[:, d0 - c0 : n - c0], done[:, d0 - c0 :], ((0,), (0,)))
            work[rest:, d0 : n + end] = work[rest:, d0 : n + end] - term[rest - d0 :, :]


def inverse_factor(gram):
    return pl.pallas_call(
        inverse_kernel,
        out_shape=jax.ShapeDtypeStruct((RANK, RANK), jnp.float32),
        in_specs=[pl.BlockSpec(memory_space=pltpu.VMEM)],
        out_specs=pl.BlockSpec(memory_space=pltpu.VMEM),
        scratch_shapes=[pltpu.VMEM((RANK, 2 * RANK), jnp.float32)],
        compiler_params=pltpu.CompilerParams(vmem_limit_bytes=6 << 20),
        cost_estimate=pl.CostEstimate(
            flops=8 * 1000 * 1000 * 1000, bytes_accessed=1 << 20, transcendentals=0
        ),
        name="inverse_factor",
    )(gram)


def per_device(
    input_query,
    grad_query,
    input_output,
    grad_output,
    moment_query,
    moment_output,
    basis_query,
    basis_output,
):
    first = lax.axis_index("rep") == 0
    tp = lax.axis_index("tp")
    y = lax.axis_index("fsdp") // N_Z

    def split(pair):
        return jnp.where(first, pair[0], pair[1]), jnp.where(first, pair[1], pair[0])

    grads = [grad_query, grad_output]
    bases = [basis_query, basis_output]
    tokens = tokens_by_distance(input_query, input_output)

    index = jnp.stack([(tp - by) % N_TP for by in (2, 0, 1, 3)] + [lax.axis_index("rep")])
    index = index.astype(jnp.int32)
    own, up, far, down = [list(pair) for pair in zip(*tokens)]
    rows, count = own[0].shape[1], own[0].shape[0]
    shape = lambda dtype, *dims: jax.ShapeDtypeStruct(dims, dtype)
    square = shape(jnp.float32, rows, RANK)
    moments = [moment_query, moment_output]
    products = []
    for w in range(2):
        grad = grads[w] if w == 0 else lax.optimization_barrier((grads[w], up[0], down[1]))[0]
        product = jnp.dot(grad, bases[w], preferred_element_type=jnp.float32)
        products.append(lax.optimization_barrier(product.astype(jnp.bfloat16)))
    part = lambda a, at: (a, (count, RANK), lambda s, i: (i[at], 0))
    near = indexed_kernel(
        near_kernel,
        index,
        [all_of(a) for a in own + up + down]
        + [part(a, at) for at in (1, 2, 3) for a in products]
        + [all_of(a) for a in moments + bases],
        [all_of(square)] * 2,
        "near_tokens",
    )
    mine, other = indexed_kernel(
        far_kernel,
        index,
        [all_of(a) for a in far] + [part(a, 0) for a in products] + [all_of(a) for a in near],
        [all_of(square), all_of(shape(jnp.bfloat16, rows, RANK))],
        "far_tokens",
    )
    mine = mine + swap_cores(other).astype(jnp.float32)
    ordered = indexed_kernel(
        order_kernel,
        index,
        [all_of(a) for a in far + own + up + down],
        [all_of(shape(jnp.bfloat16, N_TP, count, rows))] * 2,
        "order_tokens",
    )
    mine, ordered = lax.optimization_barrier((mine.astype(jnp.bfloat16), ordered))
    buffers = [
        (
            moments[w][0].astype(jnp.float32)
            + contract_rows(ordered[w].reshape(N_TP * count, rows), grads[w])
        ).astype(jnp.bfloat16)
        for w in range(2)
    ]
    parts, buffers = lax.optimization_barrier((from_all(mine, shift_tp), buffers))
    power = total(parts)
    power_b = power.astype(jnp.bfloat16)
    powers_b = split([power_b, swap_cores(power_b)])
    mine, other = split(
        [contract_rows(buffers[w], powers_b[w]).astype(jnp.bfloat16) for w in range(2)]
    )
    other = swap_cores(other)

    width = mine.shape[1]
    many, few = mine.shape[0] // N_Y, RANK // N_Y
    gram = contract_rows(power, power, lax.Precision.HIGHEST).astype(jnp.bfloat16)
    half = lambda *dims: shape(jnp.bfloat16, *dims)
    packed = local_kernel(
        pack_kernel, [mine, other, gram], half(N_Y, many + few, width), "pack_quarters"
    )
    packed = exchange(packed, Y_GROUPS)
    sent = half(N_Z, (many + 2 * few) // N_Z, width)
    packed = local_kernel(sum_y_kernel, [packed], sent, "sum_over_y")
    packed = exchange(packed, Z_GROUPS)
    packed = local_kernel(sum_z_kernel, [packed], sent, "sum_over_z")

    packed = exchange(packed, Z_GROUPS)
    raw, gram = local_kernel(
        unpack_kernel,
        [packed],
        [half(N_Y, many, width), shape(jnp.float32, few, width)],
        "unpack_rows",
    )
    gram = in_order(from_all(gram, shift_y), y)
    inverse = inverse_factor(gram)
    ortho = jnp.dot(power, inverse.T, precision=lax.Precision.HIGHEST)
    orthos = split([ortho, swap_cores(ortho)])
    raw = exchange(raw, Y_GROUPS).reshape(-1, width)

    right = jnp.dot(raw, inverse.T.astype(jnp.bfloat16), preferred_element_type=jnp.float32)
    sums = from_all(jnp.sum(right * right, axis=0, keepdims=True), shift_tp)
    right_b = right.astype(jnp.bfloat16)
    rights = split([right_b, swap_cores(right_b)])
    nexts = []
    for w in range(2):
        feedback = jnp.dot(
            orthos[w].astype(jnp.bfloat16), rights[w].T, preferred_element_type=jnp.float32
        )
        nexts.append(
            (buffers[w].astype(jnp.float32) - (1.0 - retain) / 2 * feedback).astype(jnp.bfloat16)[
                None
            ]
        )
    sums, nexts[0] = lax.optimization_barrier((sums, nexts[0]))
    scale = D / RANK**0.5 / jnp.sqrt(total(sums) + epsilon)
    scales = split([scale, swap_cores(scale)])
    scales, nexts[1] = lax.optimization_barrier((scales, nexts[1]))
    updates = [
        jnp.dot(
            (orthos[w] * scales[w]).astype(jnp.bfloat16),
            rights[w].T,
            preferred_element_type=jnp.float32,
        ).astype(jnp.bfloat16)
        for w in range(2)
    ]
    return (*updates, *nexts)


def solution(mesh):
    in_specs = (
        P(("rep", "tp"), "fsdp"),
        P("rep", "tp"),
        P(("rep", "tp"), "fsdp"),
        P("rep", "tp"),
        P("rep", "fsdp", "tp"),
        P("rep", "fsdp", "tp"),
        P("tp", None),
        P("tp", None),
    )
    out_specs = (P("fsdp", "tp"), P("fsdp", "tp"), P("rep", "fsdp", "tp"), P("rep", "fsdp", "tp"))
    return jax.shard_map(
        per_device, mesh=mesh, in_specs=in_specs, out_specs=out_specs, check_vma=False
    )
```

```python
import functools

import jax
import jax.numpy as jnp
from jax import lax
from jax.experimental import pallas as pl
from jax.experimental.pallas import tpu as pltpu
from jax.sharding import PartitionSpec as P

D = 8192
RANK = 256
N_TP = 4
N_Y = 4
N_Z = 8
LANES = 128
BLOCK = 64
GROUP = 16

retain = 0.5
epsilon = 1e-06

Y_GROUPS = [[y * N_Z + z for y in range(N_Y)] for z in range(N_Z)]
Z_GROUPS = [[y * N_Z + z for z in range(N_Z)] for y in range(N_Y)]


def contract_rows(left, right, precision=None):
    return lax.dot_general(
        left,
        right,
        (((0,), (0,)), ((), ())),
        precision=precision,
        preferred_element_type=jnp.float32,
    )


def halves(x):
    high = x.astype(jnp.bfloat16)
    return high, (x - high.astype(jnp.float32)).astype(jnp.bfloat16)


def shift_tp(x, by):
    return lax.ppermute(x, "tp", [(i, (i + by) % N_TP) for i in range(N_TP)])


def shift_y(x, by):
    pairs = [
        (y * N_Z + z, (y + by) % N_Y * N_Z + z) for y in range(N_Y) for z in range(N_Z)
    ]
    return lax.ppermute(x, "fsdp", pairs)


def swap_cores(x):
    return lax.ppermute(x, "rep", [(0, 1), (1, 0)])


def from_all(x, shift):
    return [x] + [shift(x, by) for by in (1, 2, 3)]


def in_order(parts, me):
    n = len(parts)
    whole = jnp.zeros((n,) + parts[0].shape, parts[0].dtype)
    for by in range(n):
        whole = lax.dynamic_update_index_in_dim(whole, parts[by], (me - by) % n, 0)
    return whole.reshape((n * parts[0].shape[0],) + parts[0].shape[1:])


def total(parts):
    return functools.reduce(jnp.add, [part.astype(jnp.float32) for part in parts])


def tokens_by_distance(query, output):
    query_up = shift_tp(query, 1)
    output_down = shift_tp(output, 3)
    query_down = shift_tp(query, 3)
    output_up = shift_tp(output, 1)
    query_far = shift_tp(query_up, 1)
    output_far = shift_tp(output_down, 3)
    return [
        [query, query_up, query_far, query_down],
        [output, output_up, output_far, output_down],
    ]


def exchange(x, groups):
    return lax.all_to_all(x, "fsdp", 0, 0, axis_index_groups=groups)


def local_kernel(body, operands, results, name, cost=1 << 20):
    return pl.pallas_call(
        body,
        out_shape=results,
        compiler_params=pltpu.CompilerParams(vmem_limit_bytes=12 << 20),
        cost_estimate=pl.CostEstimate(flops=cost, bytes_accessed=1 << 20, transcendentals=0),
        name=name,
    )(*operands)


def near_kernel(index, *refs):
    for w in range(2):
        own, up, down, product_own, product_up, product_down, moment, basis, out = refs[w::2]
        out[...] = (
            jnp.dot(moment[0], basis[...], preferred_element_type=jnp.float32)
            + contract_rows(own[...], product_own[...])
            + contract_rows(up[...], product_up[...])
            + contract_rows(down[...], product_down[...])
        )


def far_kernel(index, *refs):
    mine, other = refs[6:]
    query, output = [
        near[...] + contract_rows(far[...], product[...])
        for far, product, near in (refs[0:6:2], refs[1:6:2])
    ]
    first = index[N_TP] == 0
    mine[...] = jnp.where(first, query, output)
    other[...] = jnp.where(first, output, query).astype(jnp.bfloat16)


def order_kernel(index, *refs):
    for w in range(2):
        far, own, up, down, out = refs[w::2]
        for at, tokens in enumerate((far, own, up, down)):
            out[pl.ds(index[at], 1)] = tokens[...][None]


def indexed_kernel(body, index, operands, results, name):
    spec = lambda block, place: pl.BlockSpec(block, place)
    return pl.pallas_call(
        body,
        grid_spec=pltpu.PrefetchScalarGridSpec(
            num_scalar_prefetch=1,
            grid=(1,),
            in_specs=[spec(block, place) for _, block, place in operands],
            out_specs=[spec(block, place) for _, block, place in results],
        ),
        out_shape=[shape for shape, _, _ in results],
        compiler_params=pltpu.CompilerParams(
            dimension_semantics=("arbitrary",), vmem_limit_bytes=24 << 20
        ),
        cost_estimate=pl.CostEstimate(flops=1 << 20, bytes_accessed=1 << 20, transcendentals=0),
        name=name,
    )(index, *[a for a, _, _ in operands])


def all_of(a):
    return (a, a.shape, lambda s, i: (0,) * len(a.shape))


def pack_kernel(term, gram, out):
    many, few = term.shape[0] // N_Y, gram.shape[0] // N_Y
    for j in range(N_Y):
        out[j, :many] = term[j * many : (j + 1) * many]
        out[j, many:] = gram[j * few : (j + 1) * few]


def both_halves(x):
    high = x.astype(jnp.bfloat16).astype(jnp.float32)
    return jnp.concatenate([high, x - high], axis=0).astype(jnp.bfloat16)


def sum_y_kernel(pieces, out):
    few = RANK // N_Y // N_Z
    many = out.shape[1] - 2 * few
    add = lambda at, size: total([pieces[j, at : at + size] for j in range(N_Y)])
    gram = add(N_Z * many, N_Z * few)
    for j in range(N_Z):
        out[j, :many] = add(j * many, many).astype(jnp.bfloat16)
        out[j, many:] = both_halves(gram[j * few : (j + 1) * few])


def sum_z_kernel(pieces, out):
    few = RANK // N_Y // N_Z
    many = out.shape[1] - 2 * few
    rows = total([pieces[j, :many] for j in range(N_Z)]).astype(jnp.bfloat16)
    gram = total([pieces[j, many:] for j in range(N_Z)])
    gram = both_halves(gram[:few] + gram[few:])
    for j in range(N_Z):
        out[j, :many] = rows
        out[j, many:] = gram


def unpack_kernel(pieces, out, gram):
    few = RANK // N_Y // N_Z
    many = pieces.shape[1] - 2 * few
    for j in range(N_Z):
        rows = pieces[j, :many]
        for k in range(N_Y):
            out[k, j * many : (j + 1) * many] = rows
        pair = pieces[j, many:].astype(jnp.float32)
        gram[j * few : (j + 1) * few] = pair[:few] + pair[few:]


def dot_halves(a, b, dims):
    (ah, al), (bh, bl) = halves(a), halves(b)
    dot = lambda x, y: lax.dot_general(
        x, y, (dims, ((), ())), preferred_element_type=jnp.float32
    )
    return dot(ah, bh) + (dot(ah, bl) + dot(al, bh))


def inverse_kernel(gram_ref, out_ref, work):
    n = RANK
    work[:, :n] = gram_ref[...]
    row = lax.broadcasted_iota(jnp.int32, (n, n), 0)
    lane = lax.broadcasted_iota(jnp.int32, (n, n), 1)
    work[:, n:] = jnp.where(row == lane, 1.0, 0.0)
    row = lax.broadcasted_iota(jnp.int32, (BLOCK, LANES), 0)
    lane = lax.broadcasted_iota(jnp.int32, (BLOCK, LANES), 1)
    for r0 in range(0, n, BLOCK):
        c0 = r0 // LANES * LANES
        q0 = r0 - c0
        rest = r0 + BLOCK
        a = work[r0:rest, c0 : c0 + LANES]
        w = jnp.where(lane == row + q0, 1.0, 0.0)
        for k0 in range(0, BLOCK, GROUP):
            columns = [
                jnp.broadcast_to(a[:, q0 + k : q0 + k + 1], (BLOCK, LANES))
                for k in range(k0, k0 + GROUP)
            ]
            for i in range(GROUP):
                k = k0 + i
                factor = jnp.where(row > k, columns[i] * (1.0 / columns[i][k : k + 1, :]), 0.0)
                for j in range(i + 1, GROUP):
                    columns[j] = columns[j] - factor * columns[j][k : k + 1, :]
                a = a - factor * a[k : k + 1, :]
                w = w - factor * w[k : k + 1, :]
        pivots = jnp.sum(jnp.where(lane == row + q0, a, 0.0), axis=1, keepdims=True)
        w = w * lax.rsqrt(pivots)
        end = (rest + LANES - 1) // LANES * LANES
        done = dot_halves(w, work[c0 : c0 + LANES, c0 : n + end], ((1,), (0,)))
        out_ref[r0:rest, :end] = done[:, n - c0 :]
        if end < n:
            out_ref[r0:rest, end:] = jnp.zeros((BLOCK, n - end), jnp.float32)
        if rest < n:
            d0 = rest // LANES * LANES
            term = dot_halves(done[:, d0 - c0 : n - c0], done[:, d0 - c0 :], ((0,), (0,)))
            work[rest:, d0 : n + end] = work[rest:, d0 : n + end] - term[rest - d0 :, :]


def inverse_factor(gram):
    return pl.pallas_call(
        inverse_kernel,
        out_shape=jax.ShapeDtypeStruct((RANK, RANK), jnp.float32),
        in_specs=[pl.BlockSpec(memory_space=pltpu.VMEM)],
        out_specs=pl.BlockSpec(memory_space=pltpu.VMEM),
        scratch_shapes=[pltpu.VMEM((RANK, 2 * RANK), jnp.float32)],
        compiler_params=pltpu.CompilerParams(vmem_limit_bytes=6 << 20),
        cost_estimate=pl.CostEstimate(
            flops=8 * 1000 * 1000 * 1000, bytes_accessed=1 << 20, transcendentals=0
        ),
        name="inverse_factor",
    )(gram)


def per_device(
    input_query,
    grad_query,
    input_output,
    grad_output,
    moment_query,
    moment_output,
    basis_query,
    basis_output,
):
    first = lax.axis_index("rep") == 0
    tp = lax.axis_index("tp")
    y = lax.axis_index("fsdp") // N_Z

    def split(pair):
        return jnp.where(first, pair[0], pair[1]), jnp.where(first, pair[1], pair[0])

    grads = [grad_query, grad_output]
    bases = [basis_query, basis_output]
    tokens = tokens_by_distance(input_query, input_output)

    index = jnp.stack([(tp - by) % N_TP for by in (2, 0, 1, 3)] + [lax.axis_index("rep")])
    index = index.astype(jnp.int32)
    own, up, far, down = [list(pair) for pair in zip(*tokens)]
    rows, count = own[0].shape[1], own[0].shape[0]
    shape = lambda dtype, *dims: jax.ShapeDtypeStruct(dims, dtype)
    square = shape(jnp.float32, rows, RANK)
    moments = [moment_query, moment_output]
    products = []
    for w in range(2):
        grad = grads[w] if w == 0 else lax.optimization_barrier((grads[w], up[0], down[1]))[0]
        product = jnp.dot(grad, bases[w], preferred_element_type=jnp.float32)
        products.append(lax.optimization_barrier(product.astype(jnp.bfloat16)))
    part = lambda a, at: (a, (count, RANK), lambda s, i: (i[at], 0))
    near = indexed_kernel(
        near_kernel,
        index,
        [all_of(a) for a in own + up + down]
        + [part(a, at) for at in (1, 2, 3) for a in products]
        + [all_of(a) for a in moments + bases],
        [all_of(square)] * 2,
        "near_tokens",
    )
    mine, other = indexed_kernel(
        far_kernel,
        index,
        [all_of(a) for a in far] + [part(a, 0) for a in products] + [all_of(a) for a in near],
        [all_of(square), all_of(shape(jnp.bfloat16, rows, RANK))],
        "far_tokens",
    )
    mine = mine + swap_cores(other).astype(jnp.float32)
    ordered = indexed_kernel(
        order_kernel,
        index,
        [all_of(a) for a in far + own + up + down],
        [all_of(shape(jnp.bfloat16, N_TP, count, rows))] * 2,
        "order_tokens",
    )
    mine, ordered = lax.optimization_barrier((mine.astype(jnp.bfloat16), ordered))
    buffers = [
        (
            moments[w][0].astype(jnp.float32)
            + contract_rows(ordered[w].reshape(N_TP * count, rows), grads[w])
        ).astype(jnp.bfloat16)
        for w in range(2)
    ]
    taken, given = split(buffers)
    parts, taken, given = lax.optimization_barrier((from_all(mine, shift_tp), taken, given))
    given = swap_cores(given)
    power = total(parts)
    power_b = power.astype(jnp.bfloat16)
    term = (contract_rows(taken, power_b) + contract_rows(given, power_b)).astype(jnp.bfloat16)

    width = term.shape[1]
    many, few = term.shape[0] // N_Y, RANK // N_Y
    gram = contract_rows(power, power, lax.Precision.HIGHEST).astype(jnp.bfloat16)
    half = lambda *dims: shape(jnp.bfloat16, *dims)
    packed = local_kernel(
        pack_kernel, [term, gram], half(N_Y, many + few, width), "pack_quarters"
    )
    packed = exchange(packed, Y_GROUPS)
    sent = half(N_Z, (many + 2 * few) // N_Z, width)
    packed = local_kernel(sum_y_kernel, [packed], sent, "sum_over_y")
    packed = exchange(packed, Z_GROUPS)
    packed = local_kernel(sum_z_kernel, [packed], sent, "sum_over_z")

    packed = exchange(packed, Z_GROUPS)
    raw, gram = local_kernel(
        unpack_kernel,
        [packed],
        [half(N_Y, many, width), shape(jnp.float32, few, width)],
        "unpack_rows",
    )
    gram = in_order(from_all(gram, shift_y), y)
    inverse = inverse_factor(gram)
    ortho = jnp.dot(power, inverse.T, precision=lax.Precision.HIGHEST)
    orthos = split([ortho, swap_cores(ortho)])
    raw = exchange(raw, Y_GROUPS).reshape(-1, width)

    right = jnp.dot(raw, inverse.T.astype(jnp.bfloat16), preferred_element_type=jnp.float32)
    sums = from_all(jnp.sum(right * right, axis=0, keepdims=True), shift_tp)
    right_b = right.astype(jnp.bfloat16)
    rights = split([right_b, swap_cores(right_b)])
    nexts = []
    for w in range(2):
        feedback = jnp.dot(
            orthos[w].astype(jnp.bfloat16), rights[w].T, preferred_element_type=jnp.float32
        )
        nexts.append(
            (buffers[w].astype(jnp.float32) - (1.0 - retain) / 2 * feedback).astype(jnp.bfloat16)[
                None
            ]
        )
    sums, nexts[0] = lax.optimization_barrier((sums, nexts[0]))
    scale = D / RANK**0.5 / jnp.sqrt(total(sums) + epsilon)
    scales = split([scale, swap_cores(scale)])
    scales, nexts[1] = lax.optimization_barrier((scales, nexts[1]))
    updates = [
        jnp.dot(
            (orthos[w] * scales[w]).astype(jnp.bfloat16),
            rights[w].T,
            preferred_element_type=jnp.float32,
        ).astype(jnp.bfloat16)
        for w in range(2)
    ]
    return (*updates, *nexts)


def solution(mesh):
    in_specs = (
        P(("rep", "tp"), "fsdp"),
        P("rep", "tp"),
        P(("rep", "tp"), "fsdp"),
        P("rep", "tp"),
        P("rep", "fsdp", "tp"),
        P("rep", "fsdp", "tp"),
        P("tp", None),
        P("tp", None),
    )
    out_specs = (P("fsdp", "tp"), P("fsdp", "tp"), P("rep", "fsdp", "tp"), P("rep", "fsdp", "tp"))
    return jax.shard_map(
        per_device, mesh=mesh, in_specs=in_specs, out_specs=out_specs, check_vma=False
    )
```

```python
import functools

import jax
import jax.numpy as jnp
from jax import lax
from jax.experimental import pallas as pl
from jax.experimental.pallas import tpu as pltpu
from jax.sharding import PartitionSpec as P

D = 8192
RANK = 256
N_TP = 4
N_Y = 4
N_Z = 8
LANES = 128
BLOCK = 64
GROUP = 16

retain = 0.5
epsilon = 1e-06

Y_GROUPS = [[y * N_Z + z for y in range(N_Y)] for z in range(N_Z)]
Z_GROUPS = [[y * N_Z + z for z in range(N_Z)] for y in range(N_Y)]


def contract_rows(left, right, precision=None):
    return lax.dot_general(
        left,
        right,
        (((0,), (0,)), ((), ())),
        precision=precision,
        preferred_element_type=jnp.float32,
    )


def halves(x):
    high = x.astype(jnp.bfloat16)
    return high, (x - high.astype(jnp.float32)).astype(jnp.bfloat16)


def shift_tp(x, by):
    return lax.ppermute(x, "tp", [(i, (i + by) % N_TP) for i in range(N_TP)])


def shift_y(x, by):
    pairs = [
        (y * N_Z + z, (y + by) % N_Y * N_Z + z) for y in range(N_Y) for z in range(N_Z)
    ]
    return lax.ppermute(x, "fsdp", pairs)


def swap_cores(x):
    return lax.ppermute(x, "rep", [(0, 1), (1, 0)])


def from_all(x, shift):
    return [x] + [shift(x, by) for by in (1, 2, 3)]


def in_order(parts, me):
    n = len(parts)
    whole = jnp.zeros((n,) + parts[0].shape, parts[0].dtype)
    for by in range(n):
        whole = lax.dynamic_update_index_in_dim(whole, parts[by], (me - by) % n, 0)
    return whole.reshape((n * parts[0].shape[0],) + parts[0].shape[1:])


def total(parts):
    return functools.reduce(jnp.add, [part.astype(jnp.float32) for part in parts])


def tokens_by_distance(query, output):
    query_up = shift_tp(query, 1)
    output_down = shift_tp(output, 3)
    query_down = shift_tp(query, 3)
    output_up = shift_tp(output, 1)
    query_far = shift_tp(query_up, 1)
    output_far = shift_tp(output_down, 3)
    return [
        [query, query_up, query_far, query_down],
        [output, output_up, output_far, output_down],
    ]


def exchange(x, groups):
    return lax.all_to_all(x, "fsdp", 0, 0, axis_index_groups=groups)


def local_kernel(body, operands, results, name, cost=1 << 20):
    return pl.pallas_call(
        body,
        out_shape=results,
        compiler_params=pltpu.CompilerParams(vmem_limit_bytes=12 << 20),
        cost_estimate=pl.CostEstimate(flops=cost, bytes_accessed=1 << 20, transcendentals=0),
        name=name,
    )(*operands)


def near_kernel(index, *refs):
    for w in range(2):
        own, up, down, product_own, product_up, product_down, moment, basis, out = refs[w::2]
        out[...] = (
            jnp.dot(moment[0], basis[...], preferred_element_type=jnp.float32)
            + contract_rows(own[...], product_own[...])
            + contract_rows(up[...], product_up[...])
            + contract_rows(down[...], product_down[...])
        )


def far_kernel(index, *refs):
    mine, other = refs[6:]
    query, output = [
        near[...] + contract_rows(far[...], product[...])
        for far, product, near in (refs[0:6:2], refs[1:6:2])
    ]
    first = index[N_TP] == 0
    mine[...] = jnp.where(first, query, output)
    other[...] = jnp.where(first, output, query).astype(jnp.bfloat16)


def choose_kernel(index, query, output, taken, given):
    first = index[N_TP] == 0
    taken[...] = jnp.where(first, query[...], output[...])
    given[...] = jnp.where(first, output[...], query[...])


def order_kernel(index, *refs):
    for w in range(2):
        far, own, up, down, out = refs[w::2]
        for at, tokens in enumerate((far, own, up, down)):
            out[pl.ds(index[at], 1)] = tokens[...][None]


def indexed_kernel(body, index, operands, results, name, limit=6):
    spec = lambda block, place: pl.BlockSpec(block, place, pipeline_mode=pl.Buffered(1))
    results = [(jax.ShapeDtypeStruct(a.shape, a.dtype), block, place) for a, block, place in results]
    return pl.pallas_call(
        body,
        grid_spec=pltpu.PrefetchScalarGridSpec(
            num_scalar_prefetch=1,
            grid=(1,),
            in_specs=[spec(block, place) for _, block, place in operands],
            out_specs=[spec(block, place) for _, block, place in results],
        ),
        out_shape=[shape for shape, _, _ in results],
        compiler_params=pltpu.CompilerParams(
            dimension_semantics=("arbitrary",), vmem_limit_bytes=limit << 20
        ),
        cost_estimate=pl.CostEstimate(flops=1 << 20, bytes_accessed=1 << 20, transcendentals=0),
        name=name,
    )(index, *[a for a, _, _ in operands])


def all_of(a):
    return (a, a.shape, lambda s, i: (0,) * len(a.shape))


def pack_kernel(term, gram, out):
    many, few = term.shape[0] // N_Y, gram.shape[0] // N_Y
    for j in range(N_Y):
        out[j, :many] = term[j * many : (j + 1) * many]
        out[j, many:] = gram[j * few : (j + 1) * few]


def both_halves(x):
    high = x.astype(jnp.bfloat16).astype(jnp.float32)
    return jnp.concatenate([high, x - high], axis=0).astype(jnp.bfloat16)


def sum_y_kernel(pieces, out):
    few = RANK // N_Y // N_Z
    many = out.shape[1] - 2 * few
    add = lambda at, size: total([pieces[j, at : at + size] for j in range(N_Y)])
    gram = add(N_Z * many, N_Z * few)
    for j in range(N_Z):
        out[j, :many] = add(j * many, many).astype(jnp.bfloat16)
        out[j, many:] = both_halves(gram[j * few : (j + 1) * few])


def sum_z_kernel(pieces, out):
    few = RANK // N_Y // N_Z
    many = out.shape[1] - 2 * few
    rows = total([pieces[j, :many] for j in range(N_Z)]).astype(jnp.bfloat16)
    gram = total([pieces[j, many:] for j in range(N_Z)])
    gram = both_halves(gram[:few] + gram[few:])
    for j in range(N_Z):
        out[j, :many] = rows
        out[j, many:] = gram


def unpack_kernel(pieces, out, gram):
    few = RANK // N_Y // N_Z
    many = pieces.shape[1] - 2 * few
    for j in range(N_Z):
        rows = pieces[j, :many]
        for k in range(N_Y):
            out[k, j * many : (j + 1) * many] = rows
        pair = pieces[j, many:].astype(jnp.float32)
        gram[j * few : (j + 1) * few] = pair[:few] + pair[few:]


def dot_halves(a, b, dims):
    (ah, al), (bh, bl) = halves(a), halves(b)
    dot = lambda x, y: lax.dot_general(
        x, y, (dims, ((), ())), preferred_element_type=jnp.float32
    )
    return dot(ah, bh) + (dot(ah, bl) + dot(al, bh))


def inverse_kernel(gram_ref, out_ref, work):
    n = RANK
    work[:, :n] = gram_ref[...]
    row = lax.broadcasted_iota(jnp.int32, (n, n), 0)
    lane = lax.broadcasted_iota(jnp.int32, (n, n), 1)
    work[:, n:] = jnp.where(row == lane, 1.0, 0.0)
    row = lax.broadcasted_iota(jnp.int32, (BLOCK, LANES), 0)
    lane = lax.broadcasted_iota(jnp.int32, (BLOCK, LANES), 1)
    for r0 in range(0, n, BLOCK):
        c0 = r0 // LANES * LANES
        q0 = r0 - c0
        rest = r0 + BLOCK
        a = work[r0:rest, c0 : c0 + LANES]
        w = jnp.where(lane == row + q0, 1.0, 0.0)
        for k0 in range(0, BLOCK, GROUP):
            columns = [
                jnp.broadcast_to(a[:, q0 + k : q0 + k + 1], (BLOCK, LANES))
                for k in range(k0, k0 + GROUP)
            ]
            for i in range(GROUP):
                k = k0 + i
                factor = jnp.where(row > k, columns[i] * (1.0 / columns[i][k : k + 1, :]), 0.0)
                for j in range(i + 1, GROUP):
                    columns[j] = columns[j] - factor * columns[j][k : k + 1, :]
                a = a - factor * a[k : k + 1, :]
                w = w - factor * w[k : k + 1, :]
        pivots = jnp.sum(jnp.where(lane == row + q0, a, 0.0), axis=1, keepdims=True)
        w = w * lax.rsqrt(pivots)
        end = (rest + LANES - 1) // LANES * LANES
        done = dot_halves(w, work[c0 : c0 + LANES, c0 : n + end], ((1,), (0,)))
        out_ref[r0:rest, :end] = done[:, n - c0 :]
        if end < n:
            out_ref[r0:rest, end:] = jnp.zeros((BLOCK, n - end), jnp.float32)
        if rest < n:
            d0 = rest // LANES * LANES
            term = dot_halves(done[:, d0 - c0 : n - c0], done[:, d0 - c0 :], ((0,), (0,)))
            work[rest:, d0 : n + end] = work[rest:, d0 : n + end] - term[rest - d0 :, :]


def inverse_factor(gram):
    return pl.pallas_call(
        inverse_kernel,
        out_shape=jax.ShapeDtypeStruct((RANK, RANK), jnp.float32),
        in_specs=[pl.BlockSpec(memory_space=pltpu.VMEM)],
        out_specs=pl.BlockSpec(memory_space=pltpu.VMEM),
        scratch_shapes=[pltpu.VMEM((RANK, 2 * RANK), jnp.float32)],
        compiler_params=pltpu.CompilerParams(vmem_limit_bytes=6 << 20),
        cost_estimate=pl.CostEstimate(
            flops=8 * 1000 * 1000 * 1000, bytes_accessed=1 << 20, transcendentals=0
        ),
        name="inverse_factor",
    )(gram)


def per_device(
    input_query,
    grad_query,
    input_output,
    grad_output,
    moment_query,
    moment_output,
    basis_query,
    basis_output,
):
    first = lax.axis_index("rep") == 0
    tp = lax.axis_index("tp")
    y = lax.axis_index("fsdp") // N_Z

    def split(pair):
        return jnp.where(first, pair[0], pair[1]), jnp.where(first, pair[1], pair[0])

    grads = [grad_query, grad_output]
    bases = [basis_query, basis_output]
    tokens = tokens_by_distance(input_query, input_output)

    index = jnp.stack([(tp - by) % N_TP for by in (2, 0, 1, 3)] + [lax.axis_index("rep")])
    index = index.astype(jnp.int32)
    own, up, far, down = [list(pair) for pair in zip(*tokens)]
    rows, count = own[0].shape[1], own[0].shape[0]
    shape = lambda dtype, *dims: jax.ShapeDtypeStruct(dims, dtype)
    square = shape(jnp.float32, rows, RANK)
    moments = [moment_query, moment_output]
    products = []
    for w in range(2):
        grad = grads[w] if w == 0 else lax.optimization_barrier((grads[w], up[0], down[1]))[0]
        product = jnp.dot(grad, bases[w], preferred_element_type=jnp.float32)
        products.append(lax.optimization_barrier(product.astype(jnp.bfloat16)))
    part = lambda a, at: (a, (count, RANK), lambda s, i: (i[at], 0))
    near = indexed_kernel(
        near_kernel,
        index,
        [all_of(a) for a in own + up + down]
        + [part(a, at) for at in (1, 2, 3) for a in products]
        + [all_of(a) for a in moments + bases],
        [all_of(square)] * 2,
        "near_tokens",
        limit=12,
    )
    mine, other = indexed_kernel(
        far_kernel,
        index,
        [all_of(a) for a in far] + [part(a, 0) for a in products] + [all_of(a) for a in near],
        [all_of(square), all_of(shape(jnp.bfloat16, rows, RANK))],
        "far_tokens",
    )
    mine = mine + swap_cores(other).astype(jnp.float32)
    ordered = indexed_kernel(
        order_kernel,
        index,
        [all_of(a) for a in far + own + up + down],
        [all_of(shape(jnp.bfloat16, N_TP, count, rows))] * 2,
        "order_tokens",
    )
    mine, ordered = lax.optimization_barrier((mine.astype(jnp.bfloat16), ordered))
    buffers = [
        (
            moments[w][0].astype(jnp.float32)
            + contract_rows(ordered[w].reshape(N_TP * count, rows), grads[w])
        ).astype(jnp.bfloat16)
        for w in range(2)
    ]
    taken, given = indexed_kernel(
        choose_kernel,
        index,
        [all_of(a) for a in buffers],
        [all_of(a) for a in buffers],
        "choose_buffers",
    )
    parts, taken, given = lax.optimization_barrier((from_all(mine, shift_tp), taken, given))
    given = swap_cores(given)
    power = total(parts)
    power_b = power.astype(jnp.bfloat16)
    term = (contract_rows(taken, power_b) + contract_rows(given, power_b)).astype(jnp.bfloat16)

    width = term.shape[1]
    many, few = term.shape[0] // N_Y, RANK // N_Y
    gram = contract_rows(power, power, lax.Precision.HIGHEST).astype(jnp.bfloat16)
    half = lambda *dims: shape(jnp.bfloat16, *dims)
    packed = local_kernel(
        pack_kernel, [term, gram], half(N_Y, many + few, width), "pack_quarters"
    )
    packed = exchange(packed, Y_GROUPS)
    sent = half(N_Z, (many + 2 * few) // N_Z, width)
    packed = local_kernel(sum_y_kernel, [packed], sent, "sum_over_y")
    packed = exchange(packed, Z_GROUPS)
    packed = local_kernel(sum_z_kernel, [packed], sent, "sum_over_z")

    packed = exchange(packed, Z_GROUPS)
    raw, gram = local_kernel(
        unpack_kernel,
        [packed],
        [half(N_Y, many, width), shape(jnp.float32, few, width)],
        "unpack_rows",
    )
    gram = in_order(from_all(gram, shift_y), y)
    inverse = inverse_factor(gram)
    ortho = jnp.dot(power, inverse.T, precision=lax.Precision.HIGHEST)
    orthos = split([ortho, swap_cores(ortho)])
    raw = exchange(raw, Y_GROUPS).reshape(-1, width)

    right = jnp.dot(raw, inverse.T.astype(jnp.bfloat16), preferred_element_type=jnp.float32)
    sums = from_all(jnp.sum(right * right, axis=0, keepdims=True), shift_tp)
    right_b = right.astype(jnp.bfloat16)
    rights = split([right_b, swap_cores(right_b)])
    nexts = []
    for w in range(2):
        feedback = jnp.dot(
            orthos[w].astype(jnp.bfloat16), rights[w].T, preferred_element_type=jnp.float32
        )
        nexts.append(
            (buffers[w].astype(jnp.float32) - (1.0 - retain) / 2 * feedback).astype(jnp.bfloat16)[
                None
            ]
        )
    sums, nexts[0] = lax.optimization_barrier((sums, nexts[0]))
    scale = D / RANK**0.5 / jnp.sqrt(total(sums) + epsilon)
    scales = split([scale, swap_cores(scale)])
    scales, nexts[1] = lax.optimization_barrier((scales, nexts[1]))
    updates = [
        jnp.dot(
            (orthos[w] * scales[w]).astype(jnp.bfloat16),
            rights[w].T,
            preferred_element_type=jnp.float32,
        ).astype(jnp.bfloat16)
        for w in range(2)
    ]
    return (*updates, *nexts)


def solution(mesh):
    in_specs = (
        P(("rep", "tp"), "fsdp"),
        P("rep", "tp"),
        P(("rep", "tp"), "fsdp"),
        P("rep", "tp"),
        P("rep", "fsdp", "tp"),
        P("rep", "fsdp", "tp"),
        P("tp", None),
        P("tp", None),
    )
    out_specs = (P("fsdp", "tp"), P("fsdp", "tp"), P("rep", "fsdp", "tp"), P("rep", "fsdp", "tp"))
    return jax.shard_map(
        per_device, mesh=mesh, in_specs=in_specs, out_specs=out_specs, check_vma=False
    )
```

```python
import functools

import jax
import jax.numpy as jnp
from jax import lax
from jax.experimental import pallas as pl
from jax.experimental.pallas import tpu as pltpu
from jax.sharding import PartitionSpec as P

D = 8192
RANK = 256
N_TP = 4
N_Y = 4
N_Z = 8
LANES = 128
BLOCK = 64
GROUP = 16

retain = 0.5
epsilon = 1e-06

Y_GROUPS = [[y * N_Z + z for y in range(N_Y)] for z in range(N_Z)]
Z_GROUPS = [[y * N_Z + z for z in range(N_Z)] for y in range(N_Y)]


def contract_rows(left, right, precision=None):
    return lax.dot_general(
        left,
        right,
        (((0,), (0,)), ((), ())),
        precision=precision,
        preferred_element_type=jnp.float32,
    )


def halves(x):
    high = x.astype(jnp.bfloat16)
    return high, (x - high.astype(jnp.float32)).astype(jnp.bfloat16)


def shift_tp(x, by):
    return lax.ppermute(x, "tp", [(i, (i + by) % N_TP) for i in range(N_TP)])


def shift_y(x, by):
    pairs = [
        (y * N_Z + z, (y + by) % N_Y * N_Z + z) for y in range(N_Y) for z in range(N_Z)
    ]
    return lax.ppermute(x, "fsdp", pairs)


def swap_cores(x):
    return lax.ppermute(x, "rep", [(0, 1), (1, 0)])


def from_all(x, shift):
    return [x] + [shift(x, by) for by in (1, 2, 3)]


def in_order(parts, me):
    n = len(parts)
    whole = jnp.zeros((n,) + parts[0].shape, parts[0].dtype)
    for by in range(n):
        whole = lax.dynamic_update_index_in_dim(whole, parts[by], (me - by) % n, 0)
    return whole.reshape((n * parts[0].shape[0],) + parts[0].shape[1:])


def total(parts):
    return functools.reduce(jnp.add, [part.astype(jnp.float32) for part in parts])


def tokens_by_distance(query, output):
    query_up = shift_tp(query, 1)
    output_down = shift_tp(output, 3)
    query_down = shift_tp(query, 3)
    output_up = shift_tp(output, 1)
    query_far = shift_tp(query_up, 1)
    output_far = shift_tp(output_down, 3)
    return [
        [query, query_up, query_far, query_down],
        [output, output_up, output_far, output_down],
    ]


def exchange(x, groups):
    return lax.all_to_all(x, "fsdp", 0, 0, axis_index_groups=groups)


def local_kernel(body, operands, results, name, cost=1 << 20):
    return pl.pallas_call(
        body,
        out_shape=results,
        compiler_params=pltpu.CompilerParams(vmem_limit_bytes=12 << 20),
        cost_estimate=pl.CostEstimate(flops=cost, bytes_accessed=1 << 20, transcendentals=0),
        name=name,
    )(*operands)


def near_kernel(index, *refs):
    for w in range(2):
        own, up, down, product_own, product_up, product_down, moment, basis, out = refs[w::2]
        out[...] = (
            jnp.dot(moment[0], basis[...], preferred_element_type=jnp.float32)
            + contract_rows(own[...], product_own[...])
            + contract_rows(up[...], product_up[...])
            + contract_rows(down[...], product_down[...])
        )


def far_kernel(index, *refs):
    mine, other = refs[6:]
    query, output = [
        near[...] + contract_rows(far[...], product[...])
        for far, product, near in (refs[0:6:2], refs[1:6:2])
    ]
    first = index[N_TP] == 0
    mine[...] = jnp.where(first, query, output)
    other[...] = jnp.where(first, output, query).astype(jnp.bfloat16)


def order_kernel(index, *refs):
    for w in range(2):
        far, own, up, down, out = refs[w::2]
        for at, tokens in enumerate((far, own, up, down)):
            out[pl.ds(index[at], 1)] = tokens[...][None]


def indexed_kernel(body, index, operands, results, name, limit=6):
    spec = lambda block, place: pl.BlockSpec(block, place, pipeline_mode=pl.Buffered(1))
    return pl.pallas_call(
        body,
        grid_spec=pltpu.PrefetchScalarGridSpec(
            num_scalar_prefetch=1,
            grid=(1,),
            in_specs=[spec(block, place) for _, block, place in operands],
            out_specs=[spec(block, place) for _, block, place in results],
        ),
        out_shape=[shape for shape, _, _ in results],
        compiler_params=pltpu.CompilerParams(
            dimension_semantics=("arbitrary",), vmem_limit_bytes=limit << 20
        ),
        cost_estimate=pl.CostEstimate(flops=1 << 20, bytes_accessed=1 << 20, transcendentals=0),
        name=name,
    )(index, *[a for a, _, _ in operands])


def all_of(a):
    return (a, a.shape, lambda s, i: (0,) * len(a.shape))


def pack_kernel(index, term, gram, *outs):
    many, few = term.shape[0] // N_Y, gram.shape[0] // N_Y
    for by, out in enumerate(outs):
        at = index[N_TP + 1 + by]
        rows_at = pl.ds(pl.multiple_of(at * many, many), many)
        out[:many] = term[rows_at]
        out[many:] = gram[pl.ds(pl.multiple_of(at * few, few), few)]


def both_halves(x):
    high = x.astype(jnp.bfloat16).astype(jnp.float32)
    return jnp.concatenate([high, x - high], axis=0).astype(jnp.bfloat16)


def sum_y_kernel(*refs):
    *pieces, out = refs
    few = RANK // N_Y // N_Z
    many = out.shape[1] - 2 * few
    add = lambda at, size: total([piece[at : at + size] for piece in pieces])
    gram = add(N_Z * many, N_Z * few)
    for j in range(N_Z):
        out[j, :many] = add(j * many, many).astype(jnp.bfloat16)
        out[j, many:] = both_halves(gram[j * few : (j + 1) * few])


def sum_z_kernel(pieces, out):
    few = RANK // N_Y // N_Z
    many = out.shape[1] - 2 * few
    rows = total([pieces[j, :many] for j in range(N_Z)]).astype(jnp.bfloat16)
    gram = total([pieces[j, many:] for j in range(N_Z)])
    gram = both_halves(gram[:few] + gram[few:])
    for j in range(N_Z):
        out[j, :many] = rows
        out[j, many:] = gram


def unpack_kernel(pieces, out, gram):
    few = RANK // N_Y // N_Z
    many = pieces.shape[1] - 2 * few
    for j in range(N_Z):
        rows = pieces[j, :many]
        for k in range(N_Y):
            out[k, j * many : (j + 1) * many] = rows
        pair = pieces[j, many:].astype(jnp.float32)
        gram[j * few : (j + 1) * few] = pair[:few] + pair[few:]


def dot_halves(a, b, dims):
    (ah, al), (bh, bl) = halves(a), halves(b)
    dot = lambda x, y: lax.dot_general(
        x, y, (dims, ((), ())), preferred_element_type=jnp.float32
    )
    return dot(ah, bh) + (dot(ah, bl) + dot(al, bh))


def inverse_kernel(gram_ref, out_ref, work):
    n = RANK
    work[:, :n] = gram_ref[...]
    row = lax.broadcasted_iota(jnp.int32, (n, n), 0)
    lane = lax.broadcasted_iota(jnp.int32, (n, n), 1)
    work[:, n:] = jnp.where(row == lane, 1.0, 0.0)
    row = lax.broadcasted_iota(jnp.int32, (BLOCK, LANES), 0)
    lane = lax.broadcasted_iota(jnp.int32, (BLOCK, LANES), 1)
    for r0 in range(0, n, BLOCK):
        c0 = r0 // LANES * LANES
        q0 = r0 - c0
        rest = r0 + BLOCK
        a = work[r0:rest, c0 : c0 + LANES]
        w = jnp.where(lane == row + q0, 1.0, 0.0)
        for k0 in range(0, BLOCK, GROUP):
            columns = [
                jnp.broadcast_to(a[:, q0 + k : q0 + k + 1], (BLOCK, LANES))
                for k in range(k0, k0 + GROUP)
            ]
            for i in range(GROUP):
                k = k0 + i
                factor = jnp.where(row > k, columns[i] * (1.0 / columns[i][k : k + 1, :]), 0.0)
                for j in range(i + 1, GROUP):
                    columns[j] = columns[j] - factor * columns[j][k : k + 1, :]
                a = a - factor * a[k : k + 1, :]
                w = w - factor * w[k : k + 1, :]
        pivots = jnp.sum(jnp.where(lane == row + q0, a, 0.0), axis=1, keepdims=True)
        w = w * lax.rsqrt(pivots)
        end = (rest + LANES - 1) // LANES * LANES
        done = dot_halves(w, work[c0 : c0 + LANES, c0 : n + end], ((1,), (0,)))
        out_ref[r0:rest, :end] = done[:, n - c0 :]
        if end < n:
            out_ref[r0:rest, end:] = jnp.zeros((BLOCK, n - end), jnp.float32)
        if rest < n:
            d0 = rest // LANES * LANES
            term = dot_halves(done[:, d0 - c0 : n - c0], done[:, d0 - c0 :], ((0,), (0,)))
            work[rest:, d0 : n + end] = work[rest:, d0 : n + end] - term[rest - d0 :, :]


def inverse_factor(gram):
    return pl.pallas_call(
        inverse_kernel,
        out_shape=jax.ShapeDtypeStruct((RANK, RANK), jnp.float32),
        in_specs=[pl.BlockSpec(memory_space=pltpu.VMEM)],
        out_specs=pl.BlockSpec(memory_space=pltpu.VMEM),
        scratch_shapes=[pltpu.VMEM((RANK, 2 * RANK), jnp.float32)],
        compiler_params=pltpu.CompilerParams(vmem_limit_bytes=6 << 20),
        cost_estimate=pl.CostEstimate(
            flops=8 * 1000 * 1000 * 1000, bytes_accessed=1 << 20, transcendentals=0
        ),
        name="inverse_factor",
    )(gram)


def per_device(
    input_query,
    grad_query,
    input_output,
    grad_output,
    moment_query,
    moment_output,
    basis_query,
    basis_output,
):
    first = lax.axis_index("rep") == 0
    tp = lax.axis_index("tp")
    y = lax.axis_index("fsdp") // N_Z

    def split(pair):
        return jnp.where(first, pair[0], pair[1]), jnp.where(first, pair[1], pair[0])

    grads = [grad_query, grad_output]
    bases = [basis_query, basis_output]
    tokens = tokens_by_distance(input_query, input_output)

    index = jnp.stack(
        [(tp - by) % N_TP for by in (2, 0, 1, 3)]
        + [lax.axis_index("rep")]
        + [(y + by) % N_Y for by in range(N_Y)]
    )
    index = index.astype(jnp.int32)
    own, up, far, down = [list(pair) for pair in zip(*tokens)]
    rows, count = own[0].shape[1], own[0].shape[0]
    shape = lambda dtype, *dims: jax.ShapeDtypeStruct(dims, dtype)
    square = shape(jnp.float32, rows, RANK)
    moments = [moment_query, moment_output]
    products = []
    for w in range(2):
        grad = grads[w] if w == 0 else lax.optimization_barrier((grads[w], up[0], down[1]))[0]
        product = jnp.dot(grad, bases[w], preferred_element_type=jnp.float32)
        products.append(lax.optimization_barrier(product.astype(jnp.bfloat16)))
    part = lambda a, at: (a, (count, RANK), lambda s, i: (i[at], 0))
    near = indexed_kernel(
        near_kernel,
        index,
        [all_of(a) for a in own + up + down]
        + [part(a, at) for at in (1, 2, 3) for a in products]
        + [all_of(a) for a in moments + bases],
        [all_of(square)] * 2,
        "near_tokens",
        limit=12,
    )
    mine, other = indexed_kernel(
        far_kernel,
        index,
        [all_of(a) for a in far] + [part(a, 0) for a in products] + [all_of(a) for a in near],
        [all_of(square), all_of(shape(jnp.bfloat16, rows, RANK))],
        "far_tokens",
    )
    mine = mine + swap_cores(other).astype(jnp.float32)
    ordered = indexed_kernel(
        order_kernel,
        index,
        [all_of(a) for a in far + own + up + down],
        [all_of(shape(jnp.bfloat16, N_TP, count, rows))] * 2,
        "order_tokens",
    )
    mine, ordered = lax.optimization_barrier((mine.astype(jnp.bfloat16), ordered))
    buffers = [
        (
            moments[w][0].astype(jnp.float32)
            + contract_rows(ordered[w].reshape(N_TP * count, rows), grads[w])
        ).astype(jnp.bfloat16)
        for w in range(2)
    ]
    parts, buffers = lax.optimization_barrier((from_all(mine, shift_tp), buffers))
    taken, _ = split(buffers)
    given = jnp.where(first, *[swap_cores(x) for x in buffers])
    power = total(parts)
    power_b = power.astype(jnp.bfloat16)
    term = (contract_rows(taken, power_b) + contract_rows(given, power_b)).astype(jnp.bfloat16)

    width = term.shape[1]
    many, few = term.shape[0] // N_Y, RANK // N_Y
    gram = contract_rows(power, power, lax.Precision.HIGHEST).astype(jnp.bfloat16)
    half = lambda *dims: shape(jnp.bfloat16, *dims)
    packed = indexed_kernel(
        pack_kernel,
        index,
        [all_of(a) for a in (term, gram)],
        [all_of(half(many + few, width))] * N_Y,
        "pack_quarters",
    )
    packed = [packed[0]] + [shift_y(packed[by], by) for by in (1, 2, 3)]
    sent = half(N_Z, (many + 2 * few) // N_Z, width)
    packed = local_kernel(sum_y_kernel, packed, sent, "sum_over_y")
    packed = exchange(packed, Z_GROUPS)
    packed = local_kernel(sum_z_kernel, [packed], sent, "sum_over_z")

    packed = exchange(packed, Z_GROUPS)
    raw, gram = local_kernel(
        unpack_kernel,
        [packed],
        [half(N_Y, many, width), shape(jnp.float32, few, width)],
        "unpack_rows",
    )
    gram = in_order(from_all(gram, shift_y), y)
    inverse = inverse_factor(gram)
    ortho = jnp.dot(power, inverse.T, precision=lax.Precision.HIGHEST)
    orthos = split([ortho, swap_cores(ortho)])
    raw = exchange(raw, Y_GROUPS).reshape(-1, width)

    right = jnp.dot(raw, inverse.T.astype(jnp.bfloat16), preferred_element_type=jnp.float32)
    sums = from_all(jnp.sum(right * right, axis=0, keepdims=True), shift_tp)
    right_b = right.astype(jnp.bfloat16)
    rights = split([right_b, swap_cores(right_b)])
    nexts = []
    for w in range(2):
        feedback = jnp.dot(
            orthos[w].astype(jnp.bfloat16), rights[w].T, preferred_element_type=jnp.float32
        )
        nexts.append(
            (buffers[w].astype(jnp.float32) - (1.0 - retain) / 2 * feedback).astype(jnp.bfloat16)[
                None
            ]
        )
    sums, nexts[0] = lax.optimization_barrier((sums, nexts[0]))
    scale = D / RANK**0.5 / jnp.sqrt(total(sums) + epsilon)
    scales = split([scale, swap_cores(scale)])
    scales, nexts[1] = lax.optimization_barrier((scales, nexts[1]))
    updates = [
        jnp.dot(
            (orthos[w] * scales[w]).astype(jnp.bfloat16),
            rights[w].T,
            preferred_element_type=jnp.float32,
        ).astype(jnp.bfloat16)
        for w in range(2)
    ]
    return (*updates, *nexts)


def solution(mesh):
    in_specs = (
        P(("rep", "tp"), "fsdp"),
        P("rep", "tp"),
        P(("rep", "tp"), "fsdp"),
        P("rep", "tp"),
        P("rep", "fsdp", "tp"),
        P("rep", "fsdp", "tp"),
        P("tp", None),
        P("tp", None),
    )
    out_specs = (P("fsdp", "tp"), P("fsdp", "tp"), P("rep", "fsdp", "tp"), P("rep", "fsdp", "tp"))
    return jax.shard_map(
        per_device, mesh=mesh, in_specs=in_specs, out_specs=out_specs, check_vma=False
    )
```

```python
import functools

import jax
import jax.numpy as jnp
from jax import lax
from jax.experimental import pallas as pl
from jax.experimental.pallas import tpu as pltpu
from jax.sharding import PartitionSpec as P

D = 8192
RANK = 256
N_TP = 4
N_Y = 4
N_Z = 8
LANES = 128
BLOCK = 64
GROUP = 16

retain = 0.5
epsilon = 1e-06

Y_GROUPS = [[y * N_Z + z for y in range(N_Y)] for z in range(N_Z)]
Z_GROUPS = [[y * N_Z + z for z in range(N_Z)] for y in range(N_Y)]


def contract_rows(left, right, precision=None):
    return lax.dot_general(
        left,
        right,
        (((0,), (0,)), ((), ())),
        precision=precision,
        preferred_element_type=jnp.float32,
    )


def halves(x):
    high = x.astype(jnp.bfloat16)
    return high, (x - high.astype(jnp.float32)).astype(jnp.bfloat16)


def shift_tp(x, by):
    return lax.ppermute(x, "tp", [(i, (i + by) % N_TP) for i in range(N_TP)])


def shift_y(x, by):
    pairs = [
        (y * N_Z + z, (y + by) % N_Y * N_Z + z) for y in range(N_Y) for z in range(N_Z)
    ]
    return lax.ppermute(x, "fsdp", pairs)


def swap_cores(x):
    return lax.ppermute(x, "rep", [(0, 1), (1, 0)])


def from_all(x, shift):
    return [x] + [shift(x, by) for by in (1, 2, 3)]


def in_order(parts, me):
    n = len(parts)
    whole = jnp.zeros((n,) + parts[0].shape, parts[0].dtype)
    for by in range(n):
        whole = lax.dynamic_update_index_in_dim(whole, parts[by], (me - by) % n, 0)
    return whole.reshape((n * parts[0].shape[0],) + parts[0].shape[1:])


def total(parts):
    return functools.reduce(jnp.add, [part.astype(jnp.float32) for part in parts])


def tokens_by_distance(query, output):
    query_up = shift_tp(query, 1)
    output_down = shift_tp(output, 3)
    query_down = shift_tp(query, 3)
    output_up = shift_tp(output, 1)
    query_far = shift_tp(query_up, 1)
    output_far = shift_tp(output_down, 3)
    return [
        [query, query_up, query_far, query_down],
        [output, output_up, output_far, output_down],
    ]


def exchange(x, groups):
    return lax.all_to_all(x, "fsdp", 0, 0, axis_index_groups=groups)


def local_kernel(body, operands, results, name, cost=1 << 20):
    return pl.pallas_call(
        body,
        out_shape=results,
        compiler_params=pltpu.CompilerParams(vmem_limit_bytes=12 << 20),
        cost_estimate=pl.CostEstimate(flops=cost, bytes_accessed=1 << 20, transcendentals=0),
        name=name,
    )(*operands)


def near_kernel(index, *refs):
    for w in range(2):
        own, up, down, product_own, product_up, product_down, moment, basis, out = refs[w::2]
        out[...] = (
            jnp.dot(moment[0], basis[...], preferred_element_type=jnp.float32)
            + contract_rows(own[...], product_own[...])
            + contract_rows(up[...], product_up[...])
            + contract_rows(down[...], product_down[...])
        )


def far_kernel(index, *refs):
    mine, other = refs[6:]
    query, output = [
        near[...] + contract_rows(far[...], product[...])
        for far, product, near in (refs[0:6:2], refs[1:6:2])
    ]
    first = index[N_TP] == 0
    mine[...] = jnp.where(first, query, output)
    other[...] = jnp.where(first, output, query).astype(jnp.bfloat16)


def order_kernel(index, *refs):
    for w in range(2):
        far, own, up, down, out = refs[w::2]
        for at, tokens in enumerate((far, own, up, down)):
            out[pl.ds(index[at], 1)] = tokens[...][None]


def indexed_kernel(body, index, operands, results, name):
    spec = lambda block, place: pl.BlockSpec(block, place)
    return pl.pallas_call(
        body,
        grid_spec=pltpu.PrefetchScalarGridSpec(
            num_scalar_prefetch=1,
            grid=(1,),
            in_specs=[spec(block, place) for _, block, place in operands],
            out_specs=[spec(block, place) for _, block, place in results],
        ),
        out_shape=[shape for shape, _, _ in results],
        compiler_params=pltpu.CompilerParams(
            dimension_semantics=("arbitrary",), vmem_limit_bytes=24 << 20
        ),
        cost_estimate=pl.CostEstimate(flops=1 << 20, bytes_accessed=1 << 20, transcendentals=0),
        name=name,
    )(index, *[a for a, _, _ in operands])


def all_of(a):
    return (a, a.shape, lambda s, i: (0,) * len(a.shape))


def pack_kernel(index, mine, other, gram, *outs):
    many, few = mine.shape[0] // N_Y, gram.shape[0] // N_Y
    for by, out in enumerate(outs):
        at = index[N_TP + 1 + by]
        rows_at = pl.ds(pl.multiple_of(at * many, many), many)
        term = mine[rows_at].astype(jnp.float32) + other[rows_at].astype(jnp.float32)
        out[:many] = term.astype(jnp.bfloat16)
        out[many:] = gram[pl.ds(pl.multiple_of(at * few, few), few)]


def both_halves(x):
    high = x.astype(jnp.bfloat16).astype(jnp.float32)
    return jnp.concatenate([high, x - high], axis=0).astype(jnp.bfloat16)


def sum_y_kernel(*refs):
    *pieces, out = refs
    few = RANK // N_Y // N_Z
    many = out.shape[1] - 2 * few
    add = lambda at, size: total([piece[at : at + size] for piece in pieces])
    gram = add(N_Z * many, N_Z * few)
    for j in range(N_Z):
        out[j, :many] = add(j * many, many).astype(jnp.bfloat16)
        out[j, many:] = both_halves(gram[j * few : (j + 1) * few])


def sum_z_kernel(pieces, out):
    few = RANK // N_Y // N_Z
    many = out.shape[1] - 2 * few
    rows = total([pieces[j, :many] for j in range(N_Z)]).astype(jnp.bfloat16)
    gram = total([pieces[j, many:] for j in range(N_Z)])
    gram = both_halves(gram[:few] + gram[few:])
    for j in range(N_Z):
        out[j, :many] = rows
        out[j, many:] = gram


def unpack_kernel(pieces, out, gram):
    few = RANK // N_Y // N_Z
    many = pieces.shape[1] - 2 * few
    for j in range(N_Z):
        rows = pieces[j, :many]
        for k in range(N_Y):
            out[k, j * many : (j + 1) * many] = rows
        pair = pieces[j, many:].astype(jnp.float32)
        gram[j * few : (j + 1) * few] = pair[:few] + pair[few:]


def dot_halves(a, b, dims):
    (ah, al), (bh, bl) = halves(a), halves(b)
    dot = lambda x, y: lax.dot_general(
        x, y, (dims, ((), ())), preferred_element_type=jnp.float32
    )
    return dot(ah, bh) + (dot(ah, bl) + dot(al, bh))


def inverse_kernel(gram_ref, out_ref, work):
    n = RANK
    work[:, :n] = gram_ref[...]
    row = lax.broadcasted_iota(jnp.int32, (n, n), 0)
    lane = lax.broadcasted_iota(jnp.int32, (n, n), 1)
    work[:, n:] = jnp.where(row == lane, 1.0, 0.0)
    row = lax.broadcasted_iota(jnp.int32, (BLOCK, LANES), 0)
    lane = lax.broadcasted_iota(jnp.int32, (BLOCK, LANES), 1)
    for r0 in range(0, n, BLOCK):
        c0 = r0 // LANES * LANES
        q0 = r0 - c0
        rest = r0 + BLOCK
        a = work[r0:rest, c0 : c0 + LANES]
        w = jnp.where(lane == row + q0, 1.0, 0.0)
        for k0 in range(0, BLOCK, GROUP):
            columns = [
                jnp.broadcast_to(a[:, q0 + k : q0 + k + 1], (BLOCK, LANES))
                for k in range(k0, k0 + GROUP)
            ]
            for i in range(GROUP):
                k = k0 + i
                factor = jnp.where(row > k, columns[i] * (1.0 / columns[i][k : k + 1, :]), 0.0)
                for j in range(i + 1, GROUP):
                    columns[j] = columns[j] - factor * columns[j][k : k + 1, :]
                a = a - factor * a[k : k + 1, :]
                w = w - factor * w[k : k + 1, :]
        pivots = jnp.sum(jnp.where(lane == row + q0, a, 0.0), axis=1, keepdims=True)
        w = w * lax.rsqrt(pivots)
        end = (rest + LANES - 1) // LANES * LANES
        done = dot_halves(w, work[c0 : c0 + LANES, c0 : n + end], ((1,), (0,)))
        out_ref[r0:rest, :end] = done[:, n - c0 :]
        if end < n:
            out_ref[r0:rest, end:] = jnp.zeros((BLOCK, n - end), jnp.float32)
        if rest < n:
            d0 = rest // LANES * LANES
            term = dot_halves(done[:, d0 - c0 : n - c0], done[:, d0 - c0 :], ((0,), (0,)))
            work[rest:, d0 : n + end] = work[rest:, d0 : n + end] - term[rest - d0 :, :]


def inverse_factor(gram):
    return pl.pallas_call(
        inverse_kernel,
        out_shape=jax.ShapeDtypeStruct((RANK, RANK), jnp.float32),
        in_specs=[pl.BlockSpec(memory_space=pltpu.VMEM)],
        out_specs=pl.BlockSpec(memory_space=pltpu.VMEM),
        scratch_shapes=[pltpu.VMEM((RANK, 2 * RANK), jnp.float32)],
        compiler_params=pltpu.CompilerParams(vmem_limit_bytes=6 << 20),
        cost_estimate=pl.CostEstimate(
            flops=8 * 1000 * 1000 * 1000, bytes_accessed=1 << 20, transcendentals=0
        ),
        name="inverse_factor",
    )(gram)


def per_device(
    input_query,
    grad_query,
    input_output,
    grad_output,
    moment_query,
    moment_output,
    basis_query,
    basis_output,
):
    first = lax.axis_index("rep") == 0
    tp = lax.axis_index("tp")
    y = lax.axis_index("fsdp") // N_Z

    def split(pair):
        return jnp.where(first, pair[0], pair[1]), jnp.where(first, pair[1], pair[0])

    grads = [grad_query, grad_output]
    bases = [basis_query, basis_output]
    tokens = tokens_by_distance(input_query, input_output)

    index = jnp.stack(
        [(tp - by) % N_TP for by in (2, 0, 1, 3)]
        + [lax.axis_index("rep")]
        + [(y + by) % N_Y for by in range(N_Y)]
    )
    index = index.astype(jnp.int32)
    own, up, far, down = [list(pair) for pair in zip(*tokens)]
    rows, count = own[0].shape[1], own[0].shape[0]
    shape = lambda dtype, *dims: jax.ShapeDtypeStruct(dims, dtype)
    square = shape(jnp.float32, rows, RANK)
    moments = [moment_query, moment_output]
    products = []
    for w in range(2):
        grad = grads[w] if w == 0 else lax.optimization_barrier((grads[w], up[0], down[1]))[0]
        product = jnp.dot(grad, bases[w], preferred_element_type=jnp.float32)
        products.append(lax.optimization_barrier(product.astype(jnp.bfloat16)))
    part = lambda a, at: (a, (count, RANK), lambda s, i: (i[at], 0))
    near = indexed_kernel(
        near_kernel,
        index,
        [all_of(a) for a in own + up + down]
        + [part(a, at) for at in (1, 2, 3) for a in products]
        + [all_of(a) for a in moments + bases],
        [all_of(square)] * 2,
        "near_tokens",
    )
    mine, other = indexed_kernel(
        far_kernel,
        index,
        [all_of(a) for a in far] + [part(a, 0) for a in products] + [all_of(a) for a in near],
        [all_of(square), all_of(shape(jnp.bfloat16, rows, RANK))],
        "far_tokens",
    )
    mine = mine + swap_cores(other).astype(jnp.float32)
    ordered = indexed_kernel(
        order_kernel,
        index,
        [all_of(a) for a in far + own + up + down],
        [all_of(shape(jnp.bfloat16, N_TP, count, rows))] * 2,
        "order_tokens",
    )
    mine, ordered = lax.optimization_barrier((mine.astype(jnp.bfloat16), ordered))
    buffers = [
        (
            moments[w][0].astype(jnp.float32)
            + contract_rows(ordered[w].reshape(N_TP * count, rows), grads[w])
        ).astype(jnp.bfloat16)
        for w in range(2)
    ]
    parts, buffers = lax.optimization_barrier((from_all(mine, shift_tp), buffers))
    power = total(parts)
    power, power_b = lax.optimization_barrier((power, power.astype(jnp.bfloat16)))
    taken, given = split(buffers)
    mine = contract_rows(taken, power_b).astype(jnp.bfloat16)
    other = contract_rows(given, swap_cores(power_b)).astype(jnp.bfloat16)
    other = swap_cores(other)

    width = mine.shape[1]
    many, few = mine.shape[0] // N_Y, RANK // N_Y
    gram = contract_rows(power, power, lax.Precision.HIGHEST).astype(jnp.bfloat16)
    half = lambda *dims: shape(jnp.bfloat16, *dims)
    packed = indexed_kernel(
        pack_kernel,
        index,
        [all_of(a) for a in (mine, other, gram)],
        [all_of(half(many + few, width))] * N_Y,
        "pack_quarters",
    )
    packed = [packed[0]] + [shift_y(packed[by], by) for by in (1, 2, 3)]
    sent = half(N_Z, (many + 2 * few) // N_Z, width)
    packed = local_kernel(sum_y_kernel, packed, sent, "sum_over_y")
    packed = exchange(packed, Z_GROUPS)
    packed = local_kernel(sum_z_kernel, [packed], sent, "sum_over_z")

    packed = exchange(packed, Z_GROUPS)
    raw, gram = local_kernel(
        unpack_kernel,
        [packed],
        [half(N_Y, many, width), shape(jnp.float32, few, width)],
        "unpack_rows",
    )
    gram = in_order(from_all(gram, shift_y), y)
    inverse = inverse_factor(gram)
    ortho = jnp.dot(power, inverse.T, precision=lax.Precision.HIGHEST)
    orthos = split([ortho, swap_cores(ortho)])
    raw = exchange(raw, Y_GROUPS).reshape(-1, width)

    right = jnp.dot(raw, inverse.T.astype(jnp.bfloat16), preferred_element_type=jnp.float32)
    sums = from_all(jnp.sum(right * right, axis=0, keepdims=True), shift_tp)
    right_b = right.astype(jnp.bfloat16)
    rights = split([right_b, swap_cores(right_b)])
    nexts = []
    for w in range(2):
        feedback = jnp.dot(
            orthos[w].astype(jnp.bfloat16), rights[w].T, preferred_element_type=jnp.float32
        )
        nexts.append(
            (buffers[w].astype(jnp.float32) - (1.0 - retain) / 2 * feedback).astype(jnp.bfloat16)[
                None
            ]
        )
    sums, nexts[0] = lax.optimization_barrier((sums, nexts[0]))
    scale = D / RANK**0.5 / jnp.sqrt(total(sums) + epsilon)
    scales = split([scale, swap_cores(scale)])
    scales, nexts[1] = lax.optimization_barrier((scales, nexts[1]))
    updates = [
        jnp.dot(
            (orthos[w] * scales[w]).astype(jnp.bfloat16),
            rights[w].T,
            preferred_element_type=jnp.float32,
        ).astype(jnp.bfloat16)
        for w in range(2)
    ]
    return (*updates, *nexts)


def solution(mesh):
    in_specs = (
        P(("rep", "tp"), "fsdp"),
        P("rep", "tp"),
        P(("rep", "tp"), "fsdp"),
        P("rep", "tp"),
        P("rep", "fsdp", "tp"),
        P("rep", "fsdp", "tp"),
        P("tp", None),
        P("tp", None),
    )
    out_specs = (P("fsdp", "tp"), P("fsdp", "tp"), P("rep", "fsdp", "tp"), P("rep", "fsdp", "tp"))
    return jax.shard_map(
        per_device, mesh=mesh, in_specs=in_specs, out_specs=out_specs, check_vma=False
    )
```

```python
import functools

import jax
import jax.numpy as jnp
from jax import lax
from jax.experimental import pallas as pl
from jax.experimental.pallas import tpu as pltpu
from jax.sharding import PartitionSpec as P

D = 8192
RANK = 256
N_TP = 4
N_Y = 4
N_Z = 8
LANES = 128
BLOCK = 64
GROUP = 16

retain = 0.5
epsilon = 1e-06

Y_GROUPS = [[y * N_Z + z for y in range(N_Y)] for z in range(N_Z)]
Z_GROUPS = [[y * N_Z + z for z in range(N_Z)] for y in range(N_Y)]


def contract_rows(left, right, precision=None):
    return lax.dot_general(
        left,
        right,
        (((0,), (0,)), ((), ())),
        precision=precision,
        preferred_element_type=jnp.float32,
    )


def halves(x):
    high = x.astype(jnp.bfloat16)
    return high, (x - high.astype(jnp.float32)).astype(jnp.bfloat16)


def shift_tp(x, by):
    return lax.ppermute(x, "tp", [(i, (i + by) % N_TP) for i in range(N_TP)])


def shift_y(x, by):
    pairs = [
        (y * N_Z + z, (y + by) % N_Y * N_Z + z) for y in range(N_Y) for z in range(N_Z)
    ]
    return lax.ppermute(x, "fsdp", pairs)


def swap_cores(x):
    return lax.ppermute(x, "rep", [(0, 1), (1, 0)])


def from_all(x, shift):
    return [x] + [shift(x, by) for by in (1, 2, 3)]


def in_order(parts, me):
    n = len(parts)
    whole = jnp.zeros((n,) + parts[0].shape, parts[0].dtype)
    for by in range(n):
        whole = lax.dynamic_update_index_in_dim(whole, parts[by], (me - by) % n, 0)
    return whole.reshape((n * parts[0].shape[0],) + parts[0].shape[1:])


def total(parts):
    return functools.reduce(jnp.add, [part.astype(jnp.float32) for part in parts])


def tokens_by_distance(query, output):
    query_up = shift_tp(query, 1)
    output_down = shift_tp(output, 3)
    query_down = shift_tp(query, 3)
    output_up = shift_tp(output, 1)
    query_far = shift_tp(query_up, 1)
    output_far = shift_tp(output_down, 3)
    return [
        [query, query_up, query_far, query_down],
        [output, output_up, output_far, output_down],
    ]


def exchange(x, groups):
    return lax.all_to_all(x, "fsdp", 0, 0, axis_index_groups=groups)


def local_kernel(body, operands, results, name, cost=1 << 20):
    return pl.pallas_call(
        body,
        out_shape=results,
        compiler_params=pltpu.CompilerParams(vmem_limit_bytes=12 << 20),
        cost_estimate=pl.CostEstimate(flops=cost, bytes_accessed=1 << 20, transcendentals=0),
        name=name,
    )(*operands)


def near_kernel(index, *refs):
    for w in range(2):
        own, up, down, product_own, product_up, product_down, moment, basis, out = refs[w::2]
        out[...] = (
            jnp.dot(moment[0], basis[...], preferred_element_type=jnp.float32)
            + contract_rows(own[...], product_own[...])
            + contract_rows(up[...], product_up[...])
            + contract_rows(down[...], product_down[...])
        )


def far_kernel(index, *refs):
    mine, other = refs[6:]
    query, output = [
        near[...] + contract_rows(far[...], product[...])
        for far, product, near in (refs[0:6:2], refs[1:6:2])
    ]
    first = index[N_TP] == 0
    mine[...] = jnp.where(first, query, output)
    other[...] = jnp.where(first, output, query).astype(jnp.bfloat16)


def order_kernel(index, *refs):
    for w in range(2):
        far, own, up, down, out = refs[w::2]
        for at, tokens in enumerate((far, own, up, down)):
            out[pl.ds(index[at], 1)] = tokens[...][None]


def indexed_kernel(body, index, operands, results, name):
    spec = lambda block, place: pl.BlockSpec(block, place)
    return pl.pallas_call(
        body,
        grid_spec=pltpu.PrefetchScalarGridSpec(
            num_scalar_prefetch=1,
            grid=(1,),
            in_specs=[spec(block, place) for _, block, place in operands],
            out_specs=[spec(block, place) for _, block, place in results],
        ),
        out_shape=[shape for shape, _, _ in results],
        compiler_params=pltpu.CompilerParams(
            dimension_semantics=("arbitrary",), vmem_limit_bytes=24 << 20
        ),
        cost_estimate=pl.CostEstimate(flops=1 << 20, bytes_accessed=1 << 20, transcendentals=0),
        name=name,
    )(index, *[a for a, _, _ in operands])


def all_of(a):
    return (a, a.shape, lambda s, i: (0,) * len(a.shape))


def pack_kernel(mine, other, gram, out):
    many, few = mine.shape[0] // N_Y, gram.shape[0] // N_Y
    for j in range(N_Y):
        rows = slice(j * many, (j + 1) * many)
        term = mine[rows].astype(jnp.float32) + other[rows].astype(jnp.float32)
        out[j, :many] = term.astype(jnp.bfloat16)
        out[j, many:] = gram[j * few : (j + 1) * few]


def both_halves(x):
    high = x.astype(jnp.bfloat16).astype(jnp.float32)
    return jnp.concatenate([high, x - high], axis=0).astype(jnp.bfloat16)


def sum_y_kernel(pieces, out):
    few = RANK // N_Y // N_Z
    many = out.shape[1] - 2 * few
    add = lambda at, size: total([pieces[j, at : at + size] for j in range(N_Y)])
    gram = add(N_Z * many, N_Z * few)
    for j in range(N_Z):
        out[j, :many] = add(j * many, many).astype(jnp.bfloat16)
        out[j, many:] = both_halves(gram[j * few : (j + 1) * few])


def sum_z_kernel(pieces, out):
    few = RANK // N_Y // N_Z
    many = out.shape[1] - 2 * few
    rows = total([pieces[j, :many] for j in range(N_Z)]).astype(jnp.bfloat16)
    gram = total([pieces[j, many:] for j in range(N_Z)])
    gram = both_halves(gram[:few] + gram[few:])
    for j in range(N_Z):
        out[j, :many] = rows
        out[j, many:] = gram


def unpack_kernel(pieces, out, gram):
    few = RANK // N_Y // N_Z
    many = pieces.shape[1] - 2 * few
    for j in range(N_Z):
        rows = pieces[j, :many]
        for k in range(N_Y):
            out[k, j * many : (j + 1) * many] = rows
        pair = pieces[j, many:].astype(jnp.float32)
        gram[j * few : (j + 1) * few] = pair[:few] + pair[few:]


def dot_halves(a, b, dims):
    (ah, al), (bh, bl) = halves(a), halves(b)
    dot = lambda x, y: lax.dot_general(
        x, y, (dims, ((), ())), preferred_element_type=jnp.float32
    )
    return dot(ah, bh) + (dot(ah, bl) + dot(al, bh))


def inverse_kernel(gram_ref, out_ref, work):
    n = RANK
    work[:, :n] = gram_ref[...]
    row = lax.broadcasted_iota(jnp.int32, (n, n), 0)
    lane = lax.broadcasted_iota(jnp.int32, (n, n), 1)
    work[:, n:] = jnp.where(row == lane, 1.0, 0.0)
    row = lax.broadcasted_iota(jnp.int32, (BLOCK, LANES), 0)
    lane = lax.broadcasted_iota(jnp.int32, (BLOCK, LANES), 1)
    for r0 in range(0, n, BLOCK):
        c0 = r0 // LANES * LANES
        q0 = r0 - c0
        rest = r0 + BLOCK
        a = work[r0:rest, c0 : c0 + LANES]
        w = jnp.where(lane == row + q0, 1.0, 0.0)
        for k0 in range(0, BLOCK, GROUP):
            columns = [
                jnp.broadcast_to(a[:, q0 + k : q0 + k + 1], (BLOCK, LANES))
                for k in range(k0, k0 + GROUP)
            ]
            for i in range(GROUP):
                k = k0 + i
                factor = jnp.where(row > k, columns[i] * (1.0 / columns[i][k : k + 1, :]), 0.0)
                for j in range(i + 1, GROUP):
                    columns[j] = columns[j] - factor * columns[j][k : k + 1, :]
                a = a - factor * a[k : k + 1, :]
                w = w - factor * w[k : k + 1, :]
        pivots = jnp.sum(jnp.where(lane == row + q0, a, 0.0), axis=1, keepdims=True)
        w = w * lax.rsqrt(pivots)
        end = (rest + LANES - 1) // LANES * LANES
        done = dot_halves(w, work[c0 : c0 + LANES, c0 : n + end], ((1,), (0,)))
        out_ref[r0:rest, :end] = done[:, n - c0 :]
        if end < n:
            out_ref[r0:rest, end:] = jnp.zeros((BLOCK, n - end), jnp.float32)
        if rest < n:
            d0 = rest // LANES * LANES
            term = dot_halves(done[:, d0 - c0 : n - c0], done[:, d0 - c0 :], ((0,), (0,)))
            work[rest:, d0 : n + end] = work[rest:, d0 : n + end] - term[rest - d0 :, :]


def inverse_factor(gram):
    return pl.pallas_call(
        inverse_kernel,
        out_shape=jax.ShapeDtypeStruct((RANK, RANK), jnp.float32),
        in_specs=[pl.BlockSpec(memory_space=pltpu.VMEM)],
        out_specs=pl.BlockSpec(memory_space=pltpu.VMEM),
        scratch_shapes=[pltpu.VMEM((RANK, 2 * RANK), jnp.float32)],
        compiler_params=pltpu.CompilerParams(vmem_limit_bytes=6 << 20),
        cost_estimate=pl.CostEstimate(
            flops=8 * 1000 * 1000 * 1000, bytes_accessed=1 << 20, transcendentals=0
        ),
        name="inverse_factor",
    )(gram)


def per_device(
    input_query,
    grad_query,
    input_output,
    grad_output,
    moment_query,
    moment_output,
    basis_query,
    basis_output,
):
    first = lax.axis_index("rep") == 0
    tp = lax.axis_index("tp")
    y = lax.axis_index("fsdp") // N_Z

    def split(pair):
        return jnp.where(first, pair[0], pair[1]), jnp.where(first, pair[1], pair[0])

    grads = [grad_query, grad_output]
    bases = [basis_query, basis_output]
    tokens = tokens_by_distance(input_query, input_output)

    index = jnp.stack([(tp - by) % N_TP for by in (2, 0, 1, 3)] + [lax.axis_index("rep")])
    index = index.astype(jnp.int32)
    own, up, far, down = [list(pair) for pair in zip(*tokens)]
    rows, count = own[0].shape[1], own[0].shape[0]
    shape = lambda dtype, *dims: jax.ShapeDtypeStruct(dims, dtype)
    square = shape(jnp.float32, rows, RANK)
    moments = [moment_query, moment_output]
    products = []
    for w in range(2):
        grad = grads[w] if w == 0 else lax.optimization_barrier((grads[w], up[0], down[1]))[0]
        product = jnp.dot(grad, bases[w], preferred_element_type=jnp.float32)
        products.append(lax.optimization_barrier(product.astype(jnp.bfloat16)))
    part = lambda a, at: (a, (count, RANK), lambda s, i: (i[at], 0))
    near = indexed_kernel(
        near_kernel,
        index,
        [all_of(a) for a in own + up + down]
        + [part(a, at) for at in (1, 2, 3) for a in products]
        + [all_of(a) for a in moments + bases],
        [all_of(square)] * 2,
        "near_tokens",
    )
    mine, other = indexed_kernel(
        far_kernel,
        index,
        [all_of(a) for a in far] + [part(a, 0) for a in products] + [all_of(a) for a in near],
        [all_of(square), all_of(shape(jnp.bfloat16, rows, RANK))],
        "far_tokens",
    )
    mine = mine + swap_cores(other).astype(jnp.float32)
    ordered = indexed_kernel(
        order_kernel,
        index,
        [all_of(a) for a in far + own + up + down],
        [all_of(shape(jnp.bfloat16, N_TP, count, rows))] * 2,
        "order_tokens",
    )
    mine, ordered = lax.optimization_barrier((mine.astype(jnp.bfloat16), ordered))
    buffers = [
        (
            moments[w][0].astype(jnp.float32)
            + contract_rows(ordered[w].reshape(N_TP * count, rows), grads[w])
        ).astype(jnp.bfloat16)
        for w in range(2)
    ]
    parts, buffers = lax.optimization_barrier((from_all(mine, shift_tp), buffers))
    power = total(parts)
    power, power_b = lax.optimization_barrier((power, power.astype(jnp.bfloat16)))
    taken, given = split(buffers)
    mine = contract_rows(taken, power_b).astype(jnp.bfloat16)
    other = contract_rows(given, swap_cores(power_b)).astype(jnp.bfloat16)
    other = swap_cores(other)

    width = mine.shape[1]
    many, few = mine.shape[0] // N_Y, RANK // N_Y
    gram = contract_rows(power, power, lax.Precision.HIGHEST).astype(jnp.bfloat16)
    half = lambda *dims: shape(jnp.bfloat16, *dims)
    packed = local_kernel(
        pack_kernel, [mine, other, gram], half(N_Y, many + few, width), "pack_quarters"
    )
    packed = exchange(packed, Y_GROUPS)
    sent = half(N_Z, (many + 2 * few) // N_Z, width)
    packed = local_kernel(sum_y_kernel, [packed], sent, "sum_over_y")
    packed = exchange(packed, Z_GROUPS)
    packed = local_kernel(sum_z_kernel, [packed], sent, "sum_over_z")

    packed = exchange(packed, Z_GROUPS)
    raw, gram = local_kernel(
        unpack_kernel,
        [packed],
        [half(N_Y, many, width), shape(jnp.float32, few, width)],
        "unpack_rows",
    )
    gram = in_order(from_all(gram, shift_y), y)
    inverse = inverse_factor(gram)
    ortho = jnp.dot(power, inverse.T, precision=lax.Precision.HIGHEST)
    orthos = split([ortho, swap_cores(ortho)])
    raw = exchange(raw, Y_GROUPS).reshape(-1, width)

    right = jnp.dot(raw, inverse.T.astype(jnp.bfloat16), preferred_element_type=jnp.float32)
    sums = from_all(jnp.sum(right * right, axis=0, keepdims=True), shift_tp)
    right_b = right.astype(jnp.bfloat16)
    rights = split([right_b, swap_cores(right_b)])
    nexts = []
    for w in range(2):
        feedback = jnp.dot(
            orthos[w].astype(jnp.bfloat16), rights[w].T, preferred_element_type=jnp.float32
        )
        nexts.append(
            (buffers[w].astype(jnp.float32) - (1.0 - retain) / 2 * feedback).astype(jnp.bfloat16)[
                None
            ]
        )
    sums, nexts[0] = lax.optimization_barrier((sums, nexts[0]))
    scale = D / RANK**0.5 / jnp.sqrt(total(sums) + epsilon)
    scales = split([scale, swap_cores(scale)])
    scales, nexts[1] = lax.optimization_barrier((scales, nexts[1]))
    updates = [
        jnp.dot(
            (orthos[w] * scales[w]).astype(jnp.bfloat16),
            rights[w].T,
            preferred_element_type=jnp.float32,
        ).astype(jnp.bfloat16)
        for w in range(2)
    ]
    return (*updates, *nexts)


def solution(mesh):
    in_specs = (
        P(("rep", "tp"), "fsdp"),
        P("rep", "tp"),
        P(("rep", "tp"), "fsdp"),
        P("rep", "tp"),
        P("rep", "fsdp", "tp"),
        P("rep", "fsdp", "tp"),
        P("tp", None),
        P("tp", None),
    )
    out_specs = (P("fsdp", "tp"), P("fsdp", "tp"), P("rep", "fsdp", "tp"), P("rep", "fsdp", "tp"))
    return jax.shard_map(
        per_device, mesh=mesh, in_specs=in_specs, out_specs=out_specs, check_vma=False
    )
```

```python
import functools

import jax
import jax.numpy as jnp
from jax import lax
from jax.experimental import pallas as pl
from jax.experimental.pallas import tpu as pltpu
from jax.sharding import PartitionSpec as P

D = 8192
RANK = 256
N_TP = 4
N_Y = 4
N_Z = 8
LANES = 128
BLOCK = 64
GROUP = 16

retain = 0.5
epsilon = 1e-06

Y_GROUPS = [[y * N_Z + z for y in range(N_Y)] for z in range(N_Z)]
Z_GROUPS = [[y * N_Z + z for z in range(N_Z)] for y in range(N_Y)]


def contract_rows(left, right, precision=None):
    return lax.dot_general(
        left,
        right,
        (((0,), (0,)), ((), ())),
        precision=precision,
        preferred_element_type=jnp.float32,
    )


def halves(x):
    high = x.astype(jnp.bfloat16)
    return high, (x - high.astype(jnp.float32)).astype(jnp.bfloat16)


def shift_tp(x, by):
    return lax.ppermute(x, "tp", [(i, (i + by) % N_TP) for i in range(N_TP)])


def shift_y(x, by):
    pairs = [
        (y * N_Z + z, (y + by) % N_Y * N_Z + z) for y in range(N_Y) for z in range(N_Z)
    ]
    return lax.ppermute(x, "fsdp", pairs)


def swap_cores(x):
    return lax.ppermute(x, "rep", [(0, 1), (1, 0)])


def from_all(x, shift):
    return [x] + [shift(x, by) for by in (1, 2, 3)]


def in_order(parts, me):
    n = len(parts)
    whole = jnp.zeros((n,) + parts[0].shape, parts[0].dtype)
    for by in range(n):
        whole = lax.dynamic_update_index_in_dim(whole, parts[by], (me - by) % n, 0)
    return whole.reshape((n * parts[0].shape[0],) + parts[0].shape[1:])


def total(parts):
    return functools.reduce(jnp.add, [part.astype(jnp.float32) for part in parts])


def tokens_by_distance(query, output):
    query_up = shift_tp(query, 1)
    output_down = shift_tp(output, 3)
    query_down = shift_tp(query, 3)
    output_up = shift_tp(output, 1)
    query_far = shift_tp(query_up, 1)
    output_far = shift_tp(output_down, 3)
    return [
        [query, query_up, query_far, query_down],
        [output, output_up, output_far, output_down],
    ]


def exchange(x, groups):
    return lax.all_to_all(x, "fsdp", 0, 0, axis_index_groups=groups)


def local_kernel(body, operands, results, name, cost=1 << 20):
    return pl.pallas_call(
        body,
        out_shape=results,
        compiler_params=pltpu.CompilerParams(vmem_limit_bytes=12 << 20),
        cost_estimate=pl.CostEstimate(flops=cost, bytes_accessed=1 << 20, transcendentals=0),
        name=name,
    )(*operands)


def near_kernel(index, *refs):
    for w in range(2):
        own, up, down, product_own, product_up, product_down, moment, basis, out = refs[w::2]
        out[...] = (
            jnp.dot(moment[0], basis[...], preferred_element_type=jnp.float32)
            + contract_rows(own[...], product_own[...])
            + contract_rows(up[...], product_up[...])
            + contract_rows(down[...], product_down[...])
        )


def far_kernel(index, *refs):
    mine, other = refs[6:]
    query, output = [
        near[...] + contract_rows(far[...], product[...])
        for far, product, near in (refs[0:6:2], refs[1:6:2])
    ]
    first = index[N_TP] == 0
    mine[...] = jnp.where(first, query, output)
    other[...] = jnp.where(first, output, query).astype(jnp.bfloat16)


def order_kernel(index, *refs):
    for w in range(2):
        far, own, up, down, out = refs[w::2]
        for at, tokens in enumerate((far, own, up, down)):
            out[pl.ds(index[at], 1)] = tokens[...][None]


def indexed_kernel(body, index, operands, results, name):
    spec = lambda block, place: pl.BlockSpec(block, place)
    return pl.pallas_call(
        body,
        grid_spec=pltpu.PrefetchScalarGridSpec(
            num_scalar_prefetch=1,
            grid=(1,),
            in_specs=[spec(block, place) for _, block, place in operands],
            out_specs=[spec(block, place) for _, block, place in results],
        ),
        out_shape=[shape for shape, _, _ in results],
        compiler_params=pltpu.CompilerParams(
            dimension_semantics=("arbitrary",), vmem_limit_bytes=24 << 20
        ),
        cost_estimate=pl.CostEstimate(flops=1 << 20, bytes_accessed=1 << 20, transcendentals=0),
        name=name,
    )(index, *[a for a, _, _ in operands])


def all_of(a):
    return (a, a.shape, lambda s, i: (0,) * len(a.shape))


def pack_kernel(mine, other, gram, out):
    many, few = mine.shape[0] // N_Y, gram.shape[0] // N_Y
    for j in range(N_Y):
        rows = slice(j * many, (j + 1) * many)
        term = mine[rows].astype(jnp.float32) + other[rows].astype(jnp.float32)
        out[j, :many] = term.astype(jnp.bfloat16)
        out[j, many:] = gram[j * few : (j + 1) * few]


def both_halves(x):
    high = x.astype(jnp.bfloat16).astype(jnp.float32)
    return jnp.concatenate([high, x - high], axis=0).astype(jnp.bfloat16)


def sum_y_kernel(pieces, out):
    few = RANK // N_Y // N_Z
    many = out.shape[1] - 2 * few
    add = lambda at, size: total([pieces[j, at : at + size] for j in range(N_Y)])
    gram = add(N_Z * many, N_Z * few)
    for j in range(N_Z):
        out[j, :many] = add(j * many, many).astype(jnp.bfloat16)
        out[j, many:] = both_halves(gram[j * few : (j + 1) * few])


def sum_z_kernel(pieces, out):
    few = RANK // N_Y // N_Z
    many = out.shape[1] - 2 * few
    rows = total([pieces[j, :many] for j in range(N_Z)]).astype(jnp.bfloat16)
    gram = total([pieces[j, many:] for j in range(N_Z)])
    gram = both_halves(gram[:few] + gram[few:])
    for j in range(N_Z):
        out[j, :many] = rows
        out[j, many:] = gram


def unpack_kernel(pieces, out, gram):
    few = RANK // N_Y // N_Z
    many = pieces.shape[1] - 2 * few
    for j in range(N_Z):
        rows = pieces[j, :many]
        for k in range(N_Y):
            out[k, j * many : (j + 1) * many] = rows
        pair = pieces[j, many:].astype(jnp.float32)
        gram[j * few : (j + 1) * few] = pair[:few] + pair[few:]


def dot_halves(a, b, dims):
    (ah, al), (bh, bl) = halves(a), halves(b)
    dot = lambda x, y: lax.dot_general(
        x, y, (dims, ((), ())), preferred_element_type=jnp.float32
    )
    return dot(ah, bh) + (dot(ah, bl) + dot(al, bh))


def inverse_kernel(gram_ref, out_ref, work):
    n = RANK
    work[:, :n] = gram_ref[...]
    row = lax.broadcasted_iota(jnp.int32, (n, n), 0)
    lane = lax.broadcasted_iota(jnp.int32, (n, n), 1)
    work[:, n:] = jnp.where(row == lane, 1.0, 0.0)
    row = lax.broadcasted_iota(jnp.int32, (BLOCK, LANES), 0)
    lane = lax.broadcasted_iota(jnp.int32, (BLOCK, LANES), 1)
    for r0 in range(0, n, BLOCK):
        c0 = r0 // LANES * LANES
        q0 = r0 - c0
        rest = r0 + BLOCK
        a = work[r0:rest, c0 : c0 + LANES]
        w = jnp.where(lane == row + q0, 1.0, 0.0)
        for k0 in range(0, BLOCK, GROUP):
            columns = [
                jnp.broadcast_to(a[:, q0 + k : q0 + k + 1], (BLOCK, LANES))
                for k in range(k0, k0 + GROUP)
            ]
            for i in range(GROUP):
                k = k0 + i
                factor = jnp.where(row > k, columns[i] * (1.0 / columns[i][k : k + 1, :]), 0.0)
                for j in range(i + 1, GROUP):
                    columns[j] = columns[j] - factor * columns[j][k : k + 1, :]
                a = a - factor * a[k : k + 1, :]
                w = w - factor * w[k : k + 1, :]
        pivots = jnp.sum(jnp.where(lane == row + q0, a, 0.0), axis=1, keepdims=True)
        w = w * lax.rsqrt(pivots)
        end = (rest + LANES - 1) // LANES * LANES
        done = dot_halves(w, work[c0 : c0 + LANES, c0 : n + end], ((1,), (0,)))
        out_ref[r0:rest, :end] = done[:, n - c0 :]
        if end < n:
            out_ref[r0:rest, end:] = jnp.zeros((BLOCK, n - end), jnp.float32)
        if rest < n:
            d0 = rest // LANES * LANES
            term = dot_halves(done[:, d0 - c0 : n - c0], done[:, d0 - c0 :], ((0,), (0,)))
            work[rest:, d0 : n + end] = work[rest:, d0 : n + end] - term[rest - d0 :, :]


def inverse_factor(gram):
    return pl.pallas_call(
        inverse_kernel,
        out_shape=jax.ShapeDtypeStruct((RANK, RANK), jnp.float32),
        in_specs=[pl.BlockSpec(memory_space=pltpu.VMEM)],
        out_specs=pl.BlockSpec(memory_space=pltpu.VMEM),
        scratch_shapes=[pltpu.VMEM((RANK, 2 * RANK), jnp.float32)],
        compiler_params=pltpu.CompilerParams(vmem_limit_bytes=6 << 20),
        cost_estimate=pl.CostEstimate(
            flops=8 * 1000 * 1000 * 1000, bytes_accessed=1 << 20, transcendentals=0
        ),
        name="inverse_factor",
    )(gram)


def per_device(
    input_query,
    grad_query,
    input_output,
    grad_output,
    moment_query,
    moment_output,
    basis_query,
    basis_output,
):
    first = lax.axis_index("rep") == 0
    tp = lax.axis_index("tp")
    y = lax.axis_index("fsdp") // N_Z

    def split(pair):
        return jnp.where(first, pair[0], pair[1]), jnp.where(first, pair[1], pair[0])

    grads = [grad_query, grad_output]
    bases = [basis_query, basis_output]
    tokens = tokens_by_distance(input_query, input_output)

    index = jnp.stack([(tp - by) % N_TP for by in (2, 0, 1, 3)] + [lax.axis_index("rep")])
    index = index.astype(jnp.int32)
    own, up, far, down = [list(pair) for pair in zip(*tokens)]
    rows, count = own[0].shape[1], own[0].shape[0]
    shape = lambda dtype, *dims: jax.ShapeDtypeStruct(dims, dtype)
    square = shape(jnp.float32, rows, RANK)
    moments = [moment_query, moment_output]
    products = []
    for w in range(2):
        grad = grads[w] if w == 0 else lax.optimization_barrier((grads[w], up[0], down[1]))[0]
        product = jnp.dot(grad, bases[w], preferred_element_type=jnp.float32)
        products.append(lax.optimization_barrier(product.astype(jnp.bfloat16)))
    part = lambda a, at: (a, (count, RANK), lambda s, i: (i[at], 0))
    near = indexed_kernel(
        near_kernel,
        index,
        [all_of(a) for a in own + up + down]
        + [part(a, at) for at in (1, 2, 3) for a in products]
        + [all_of(a) for a in moments + bases],
        [all_of(square)] * 2,
        "near_tokens",
    )
    mine, other = indexed_kernel(
        far_kernel,
        index,
        [all_of(a) for a in far] + [part(a, 0) for a in products] + [all_of(a) for a in near],
        [all_of(square), all_of(shape(jnp.bfloat16, rows, RANK))],
        "far_tokens",
    )
    mine = mine + swap_cores(other).astype(jnp.float32)
    ordered = indexed_kernel(
        order_kernel,
        index,
        [all_of(a) for a in far + own + up + down],
        [all_of(shape(jnp.bfloat16, N_TP, count, rows))] * 2,
        "order_tokens",
    )
    mine, ordered = lax.optimization_barrier((mine.astype(jnp.bfloat16), ordered))
    buffers = [
        (
            moments[w][0].astype(jnp.float32)
            + contract_rows(ordered[w].reshape(N_TP * count, rows), grads[w])
        ).astype(jnp.bfloat16)
        for w in range(2)
    ]
    parts, buffers = lax.optimization_barrier((from_all(mine, shift_tp), buffers))
    power = total(parts)
    power, power_b = lax.optimization_barrier((power, power.astype(jnp.bfloat16)))
    taken, given = split(buffers)
    mine = contract_rows(taken, power_b).astype(jnp.bfloat16)
    other = contract_rows(given, swap_cores(power_b)).astype(jnp.bfloat16)
    other = swap_cores(other)

    width = mine.shape[1]
    many, few = mine.shape[0] // N_Y, RANK // N_Y
    gram = contract_rows(power, power, lax.Precision.HIGHEST).astype(jnp.bfloat16)
    half = lambda *dims: shape(jnp.bfloat16, *dims)
    packed = local_kernel(
        pack_kernel, [mine, other, gram], half(N_Y, many + few, width), "pack_quarters"
    )
    packed = exchange(packed, Y_GROUPS)
    sent = half(N_Z, (many + 2 * few) // N_Z, width)
    packed = local_kernel(sum_y_kernel, [packed], sent, "sum_over_y")
    packed = exchange(packed, Z_GROUPS)
    packed = local_kernel(sum_z_kernel, [packed], sent, "sum_over_z")

    packed = exchange(packed, Z_GROUPS)
    raw, gram = local_kernel(
        unpack_kernel,
        [packed],
        [half(N_Y, many, width), shape(jnp.float32, few, width)],
        "unpack_rows",
    )
    gram = in_order(from_all(gram, shift_y), y)
    inverse = inverse_factor(gram)
    ortho = jnp.dot(power, inverse.T, precision=lax.Precision.HIGHEST)
    inverse, ortho = lax.optimization_barrier((inverse, ortho))
    orthos = split([ortho, swap_cores(ortho)])
    raw = exchange(raw, Y_GROUPS).reshape(-1, width)

    right = jnp.dot(raw, inverse.T.astype(jnp.bfloat16), preferred_element_type=jnp.float32)
    sums = from_all(jnp.sum(right * right, axis=0, keepdims=True), shift_tp)
    right_b = right.astype(jnp.bfloat16)
    rights = split([right_b, swap_cores(right_b)])
    nexts = []
    for w in range(2):
        feedback = jnp.dot(
            orthos[w].astype(jnp.bfloat16), rights[w].T, preferred_element_type=jnp.float32
        )
        nexts.append(
            (buffers[w].astype(jnp.float32) - (1.0 - retain) / 2 * feedback).astype(jnp.bfloat16)[
                None
            ]
        )
    sums, nexts[0] = lax.optimization_barrier((sums, nexts[0]))
    scale = D / RANK**0.5 / jnp.sqrt(total(sums) + epsilon)
    scales = split([scale, swap_cores(scale)])
    scales, nexts[1] = lax.optimization_barrier((scales, nexts[1]))
    updates = [
        jnp.dot(
            (orthos[w] * scales[w]).astype(jnp.bfloat16),
            rights[w].T,
            preferred_element_type=jnp.float32,
        ).astype(jnp.bfloat16)
        for w in range(2)
    ]
    return (*updates, *nexts)


def solution(mesh):
    in_specs = (
        P(("rep", "tp"), "fsdp"),
        P("rep", "tp"),
        P(("rep", "tp"), "fsdp"),
        P("rep", "tp"),
        P("rep", "fsdp", "tp"),
        P("rep", "fsdp", "tp"),
        P("tp", None),
        P("tp", None),
    )
    out_specs = (P("fsdp", "tp"), P("fsdp", "tp"), P("rep", "fsdp", "tp"), P("rep", "fsdp", "tp"))
    return jax.shard_map(
        per_device, mesh=mesh, in_specs=in_specs, out_specs=out_specs, check_vma=False
    )
```

```python
import functools

import jax
import jax.numpy as jnp
from jax import lax
from jax.experimental import pallas as pl
from jax.experimental.pallas import tpu as pltpu
from jax.sharding import PartitionSpec as P

D = 8192
RANK = 256
N_TP = 4
N_Y = 4
N_Z = 8
LANES = 128
BLOCK = 64
GROUP = 16

retain = 0.5
epsilon = 1e-06

Y_GROUPS = [[y * N_Z + z for y in range(N_Y)] for z in range(N_Z)]
Z_GROUPS = [[y * N_Z + z for z in range(N_Z)] for y in range(N_Y)]


def contract_rows(left, right, precision=None):
    return lax.dot_general(
        left,
        right,
        (((0,), (0,)), ((), ())),
        precision=precision,
        preferred_element_type=jnp.float32,
    )


def halves(x):
    high = x.astype(jnp.bfloat16)
    return high, (x - high.astype(jnp.float32)).astype(jnp.bfloat16)


def shift_tp(x, by):
    return lax.ppermute(x, "tp", [(i, (i + by) % N_TP) for i in range(N_TP)])


def shift_y(x, by):
    pairs = [
        (y * N_Z + z, (y + by) % N_Y * N_Z + z) for y in range(N_Y) for z in range(N_Z)
    ]
    return lax.ppermute(x, "fsdp", pairs)


def swap_cores(x):
    return lax.ppermute(x, "rep", [(0, 1), (1, 0)])


def from_all(x, shift):
    return [x] + [shift(x, by) for by in (1, 2, 3)]


def in_order(parts, me):
    n = len(parts)
    whole = jnp.zeros((n,) + parts[0].shape, parts[0].dtype)
    for by in range(n):
        whole = lax.dynamic_update_index_in_dim(whole, parts[by], (me - by) % n, 0)
    return whole.reshape((n * parts[0].shape[0],) + parts[0].shape[1:])


def total(parts):
    return functools.reduce(jnp.add, [part.astype(jnp.float32) for part in parts])


def tokens_by_distance(query, output):
    query_up = shift_tp(query, 1)
    output_down = shift_tp(output, 3)
    query_down = shift_tp(query, 3)
    output_up = shift_tp(output, 1)
    query_far = shift_tp(query_up, 1)
    output_far = shift_tp(output_down, 3)
    return [
        [query, query_up, query_far, query_down],
        [output, output_up, output_far, output_down],
    ]


def exchange(x, groups):
    return lax.all_to_all(x, "fsdp", 0, 0, axis_index_groups=groups)


def local_kernel(body, operands, results, name, cost=1 << 20):
    return pl.pallas_call(
        body,
        out_shape=results,
        compiler_params=pltpu.CompilerParams(vmem_limit_bytes=12 << 20),
        cost_estimate=pl.CostEstimate(flops=cost, bytes_accessed=1 << 20, transcendentals=0),
        name=name,
    )(*operands)


def near_kernel(index, *refs):
    for w in range(2):
        own, up, down, product_own, product_up, product_down, moment, basis, out = refs[w::2]
        out[...] = (
            jnp.dot(moment[0], basis[...], preferred_element_type=jnp.float32)
            + contract_rows(own[...], product_own[...])
            + contract_rows(up[...], product_up[...])
            + contract_rows(down[...], product_down[...])
        )


def far_kernel(index, *refs):
    mine, other = refs[6:]
    query, output = [
        near[...] + contract_rows(far[...], product[...])
        for far, product, near in (refs[0:6:2], refs[1:6:2])
    ]
    first = index[N_TP] == 0
    mine[...] = jnp.where(first, query, output)
    other[...] = jnp.where(first, output, query).astype(jnp.bfloat16)


def order_kernel(index, *refs):
    for w in range(2):
        far, own, up, down, out = refs[w::2]
        for at, tokens in enumerate((far, own, up, down)):
            out[pl.ds(index[at], 1)] = tokens[...][None]


def indexed_kernel(body, index, operands, results, name):
    spec = lambda block, place: pl.BlockSpec(block, place)
    return pl.pallas_call(
        body,
        grid_spec=pltpu.PrefetchScalarGridSpec(
            num_scalar_prefetch=1,
            grid=(1,),
            in_specs=[spec(block, place) for _, block, place in operands],
            out_specs=[spec(block, place) for _, block, place in results],
        ),
        out_shape=[shape for shape, _, _ in results],
        compiler_params=pltpu.CompilerParams(
            dimension_semantics=("arbitrary",), vmem_limit_bytes=24 << 20
        ),
        cost_estimate=pl.CostEstimate(flops=1 << 20, bytes_accessed=1 << 20, transcendentals=0),
        name=name,
    )(index, *[a for a, _, _ in operands])


def all_of(a):
    return (a, a.shape, lambda s, i: (0,) * len(a.shape))


def pack_kernel(mine, other, gram, out):
    many, few = mine.shape[0] // N_Y, gram.shape[0] // N_Y
    for j in range(N_Y):
        rows = slice(j * many, (j + 1) * many)
        term = mine[rows].astype(jnp.float32) + other[rows].astype(jnp.float32)
        out[j, :many] = term.astype(jnp.bfloat16)
        out[j, many:] = gram[j * few : (j + 1) * few]


def both_halves(x):
    high = x.astype(jnp.bfloat16).astype(jnp.float32)
    return jnp.concatenate([high, x - high], axis=0).astype(jnp.bfloat16)


def sum_y_kernel(pieces, out):
    few = RANK // N_Y // N_Z
    many = out.shape[1] - 2 * few
    add = lambda at, size: total([pieces[j, at : at + size] for j in range(N_Y)])
    gram = add(N_Z * many, N_Z * few)
    for j in range(N_Z):
        out[j, :many] = add(j * many, many).astype(jnp.bfloat16)
        out[j, many:] = both_halves(gram[j * few : (j + 1) * few])


def sum_z_kernel(pieces, out):
    few = RANK // N_Y // N_Z
    many = out.shape[1] - 2 * few
    rows = total([pieces[j, :many] for j in range(N_Z)]).astype(jnp.bfloat16)
    gram = total([pieces[j, many:] for j in range(N_Z)])
    gram = both_halves(gram[:few] + gram[few:])
    for j in range(N_Z):
        out[j, :many] = rows
        out[j, many:] = gram


def unpack_kernel(pieces, out, gram):
    few = RANK // N_Y // N_Z
    many = pieces.shape[1] - 2 * few
    for j in range(N_Z):
        rows = pieces[j, :many]
        for k in range(N_Y):
            out[k, j * many : (j + 1) * many] = rows
        pair = pieces[j, many:].astype(jnp.float32)
        gram[j * few : (j + 1) * few] = pair[:few] + pair[few:]


def dot_halves(a, b, dims):
    (ah, al), (bh, bl) = halves(a), halves(b)
    dot = lambda x, y: lax.dot_general(
        x, y, (dims, ((), ())), preferred_element_type=jnp.float32
    )
    return dot(ah, bh) + (dot(ah, bl) + dot(al, bh))


def inverse_kernel(gram_ref, out_ref, work):
    n = RANK
    work[:, :n] = gram_ref[...]
    row = lax.broadcasted_iota(jnp.int32, (n, n), 0)
    lane = lax.broadcasted_iota(jnp.int32, (n, n), 1)
    work[:, n:] = jnp.where(row == lane, 1.0, 0.0)
    row = lax.broadcasted_iota(jnp.int32, (BLOCK, LANES), 0)
    lane = lax.broadcasted_iota(jnp.int32, (BLOCK, LANES), 1)
    for r0 in range(0, n, BLOCK):
        c0 = r0 // LANES * LANES
        q0 = r0 - c0
        rest = r0 + BLOCK
        a = work[r0:rest, c0 : c0 + LANES]
        w = jnp.where(lane == row + q0, 1.0, 0.0)
        for k0 in range(0, BLOCK, GROUP):
            columns = [
                jnp.broadcast_to(a[:, q0 + k : q0 + k + 1], (BLOCK, LANES))
                for k in range(k0, k0 + GROUP)
            ]
            for i in range(GROUP):
                k = k0 + i
                factor = jnp.where(row > k, columns[i] * (1.0 / columns[i][k : k + 1, :]), 0.0)
                for j in range(i + 1, GROUP):
                    columns[j] = columns[j] - factor * columns[j][k : k + 1, :]
                a = a - factor * a[k : k + 1, :]
                w = w - factor * w[k : k + 1, :]
        pivots = jnp.sum(jnp.where(lane == row + q0, a, 0.0), axis=1, keepdims=True)
        w = w * lax.rsqrt(pivots)
        end = (rest + LANES - 1) // LANES * LANES
        done = dot_halves(w, work[c0 : c0 + LANES, c0 : n + end], ((1,), (0,)))
        out_ref[r0:rest, :end] = done[:, n - c0 :]
        if end < n:
            out_ref[r0:rest, end:] = jnp.zeros((BLOCK, n - end), jnp.float32)
        if rest < n:
            d0 = rest // LANES * LANES
            term = dot_halves(done[:, d0 - c0 : n - c0], done[:, d0 - c0 :], ((0,), (0,)))
            work[rest:, d0 : n + end] = work[rest:, d0 : n + end] - term[rest - d0 :, :]


def inverse_factor(gram):
    return pl.pallas_call(
        inverse_kernel,
        out_shape=jax.ShapeDtypeStruct((RANK, RANK), jnp.float32),
        in_specs=[pl.BlockSpec(memory_space=pltpu.VMEM)],
        out_specs=pl.BlockSpec(memory_space=pltpu.VMEM),
        scratch_shapes=[pltpu.VMEM((RANK, 2 * RANK), jnp.float32)],
        compiler_params=pltpu.CompilerParams(vmem_limit_bytes=6 << 20),
        cost_estimate=pl.CostEstimate(
            flops=8 * 1000 * 1000 * 1000, bytes_accessed=1 << 20, transcendentals=0
        ),
        name="inverse_factor",
    )(gram)


def per_device(
    input_query,
    grad_query,
    input_output,
    grad_output,
    moment_query,
    moment_output,
    basis_query,
    basis_output,
):
    first = lax.axis_index("rep") == 0
    tp = lax.axis_index("tp")
    y = lax.axis_index("fsdp") // N_Z

    def split(pair):
        return jnp.where(first, pair[0], pair[1]), jnp.where(first, pair[1], pair[0])

    grads = [grad_query, grad_output]
    bases = [basis_query, basis_output]
    tokens = tokens_by_distance(input_query, input_output)

    index = jnp.stack([(tp - by) % N_TP for by in (2, 0, 1, 3)] + [lax.axis_index("rep")])
    index = index.astype(jnp.int32)
    own, up, far, down = [list(pair) for pair in zip(*tokens)]
    rows, count = own[0].shape[1], own[0].shape[0]
    shape = lambda dtype, *dims: jax.ShapeDtypeStruct(dims, dtype)
    square = shape(jnp.float32, rows, RANK)
    moments = [moment_query, moment_output]
    products = []
    for w in range(2):
        grad = grads[w] if w == 0 else lax.optimization_barrier((grads[w], up[0], down[1]))[0]
        product = jnp.dot(grad, bases[w], preferred_element_type=jnp.float32)
        products.append(lax.optimization_barrier(product.astype(jnp.bfloat16)))
    part = lambda a, at: (a, (count, RANK), lambda s, i: (i[at], 0))
    near = indexed_kernel(
        near_kernel,
        index,
        [all_of(a) for a in own + up + down]
        + [part(a, at) for at in (1, 2, 3) for a in products]
        + [all_of(a) for a in moments + bases],
        [all_of(square)] * 2,
        "near_tokens",
    )
    mine, other = indexed_kernel(
        far_kernel,
        index,
        [all_of(a) for a in far] + [part(a, 0) for a in products] + [all_of(a) for a in near],
        [all_of(square), all_of(shape(jnp.bfloat16, rows, RANK))],
        "far_tokens",
    )
    mine = mine + swap_cores(other).astype(jnp.float32)
    ordered = indexed_kernel(
        order_kernel,
        index,
        [all_of(a) for a in far + own + up + down],
        [all_of(shape(jnp.bfloat16, N_TP, count, rows))] * 2,
        "order_tokens",
    )
    mine, ordered = lax.optimization_barrier((mine.astype(jnp.bfloat16), ordered))
    buffers = [
        (
            moments[w][0].astype(jnp.float32)
            + contract_rows(ordered[w].reshape(N_TP * count, rows), grads[w])
        ).astype(jnp.bfloat16)
        for w in range(2)
    ]
    parts, buffers = lax.optimization_barrier((from_all(mine, shift_tp), buffers))
    power = total(parts)
    power, power_b = lax.optimization_barrier((power, power.astype(jnp.bfloat16)))
    taken, given = split(buffers)
    mine = contract_rows(taken, power_b).astype(jnp.bfloat16)
    other = contract_rows(given, swap_cores(power_b)).astype(jnp.bfloat16)
    other = swap_cores(other)

    width = mine.shape[1]
    many, few = mine.shape[0] // N_Y, RANK // N_Y
    gram = contract_rows(power, power, lax.Precision.HIGHEST).astype(jnp.bfloat16)
    half = lambda *dims: shape(jnp.bfloat16, *dims)
    packed = local_kernel(
        pack_kernel, [mine, other, gram], half(N_Y, many + few, width), "pack_quarters"
    )
    packed = exchange(packed, Y_GROUPS)
    sent = half(N_Z, (many + 2 * few) // N_Z, width)
    packed = local_kernel(sum_y_kernel, [packed], sent, "sum_over_y")
    packed = exchange(packed, Z_GROUPS)
    packed = local_kernel(sum_z_kernel, [packed], sent, "sum_over_z")

    packed = exchange(packed, Z_GROUPS)
    raw, gram = local_kernel(
        unpack_kernel,
        [packed],
        [half(N_Y, many, width), shape(jnp.float32, few, width)],
        "unpack_rows",
    )
    gram = in_order(from_all(gram, shift_y), y)
    inverse = inverse_factor(gram)
    ortho = jnp.dot(power, inverse.T, precision=lax.Precision.HIGHEST)
    inverse, ortho = lax.optimization_barrier((inverse, ortho))
    orthos = [ortho, swap_cores(ortho)]
    inverse, *orthos = lax.optimization_barrier((inverse, *orthos))
    orthos = split(orthos)
    raw = exchange(raw, Y_GROUPS).reshape(-1, width)

    right = jnp.dot(raw, inverse.T.astype(jnp.bfloat16), preferred_element_type=jnp.float32)
    sums = from_all(jnp.sum(right * right, axis=0, keepdims=True), shift_tp)
    right_b = right.astype(jnp.bfloat16)
    rights = split([right_b, swap_cores(right_b)])
    nexts = []
    for w in range(2):
        feedback = jnp.dot(
            orthos[w].astype(jnp.bfloat16), rights[w].T, preferred_element_type=jnp.float32
        )
        nexts.append(
            (buffers[w].astype(jnp.float32) - (1.0 - retain) / 2 * feedback).astype(jnp.bfloat16)[
                None
            ]
        )
    sums, nexts[0] = lax.optimization_barrier((sums, nexts[0]))
    scale = D / RANK**0.5 / jnp.sqrt(total(sums) + epsilon)
    scales = split([scale, swap_cores(scale)])
    scales, nexts[1] = lax.optimization_barrier((scales, nexts[1]))
    updates = [
        jnp.dot(
            (orthos[w] * scales[w]).astype(jnp.bfloat16),
            rights[w].T,
            preferred_element_type=jnp.float32,
        ).astype(jnp.bfloat16)
        for w in range(2)
    ]
    return (*updates, *nexts)


def solution(mesh):
    in_specs = (
        P(("rep", "tp"), "fsdp"),
        P("rep", "tp"),
        P(("rep", "tp"), "fsdp"),
        P("rep", "tp"),
        P("rep", "fsdp", "tp"),
        P("rep", "fsdp", "tp"),
        P("tp", None),
        P("tp", None),
    )
    out_specs = (P("fsdp", "tp"), P("fsdp", "tp"), P("rep", "fsdp", "tp"), P("rep", "fsdp", "tp"))
    return jax.shard_map(
        per_device, mesh=mesh, in_specs=in_specs, out_specs=out_specs, check_vma=False
    )
```
